32 devices in a mesh: groups: 2 (over x), dp: 16 (over z, y, core).
Axes of the slice: x: 2, y: 2, z: 4, core: 2. Of those that a mesh axis runs over, the one named last changes fastest.
Arguments:
- tiles: bfloat16 [1024, 64, 3072], P(('groups', 'dp')), parts along dimension 0, may hold values from -6 to 6
- conv_weight: bfloat16 [3072, 768], P('dp'), may hold values from -0.109375 to 0.109375
- tile_slide: int32 [1024], P(('groups', 'dp')), parts along dimension 0, may hold values from 0 to 31, as said below
- slide_owner: int32 [64], P('groups'), parts along dimension 0, may hold values from 0 to 15, as said below
- labels: int32 [64], P('groups'), parts along dimension 0, may hold values from 0 to 1
- attn_v: bfloat16 [768, 384], replicated, may hold values from -0.21875 to 0.21875
- attn_u: bfloat16 [768, 384], replicated, may hold values from -0.21875 to 0.21875
- attn_w: float32 [384], replicated, may hold values from -0.5 to 0.5
- class_w: float32 [768, 2], replicated, may hold values from -0.6 to 0.6
Outputs:
- conv_grad: float32 [6144, 768], P(('groups', 'dp')), parts along dimension 0
- attn_v_grad: float32 [1536, 384], P(('groups', 'dp')), parts along dimension 0
- attn_u_grad: float32 [1536, 384], P(('groups', 'dp')), parts along dimension 0
- attn_w_grad: float32 [768], P('groups'), parts along dimension 0
- class_grad: float32 [1536, 2], P('groups'), parts along dimension 0
- slide_logits: float32 [64, 2], P(('groups', 'dp')), parts along dimension 0
- loss: float32 [2], P('groups'), parts along dimension 0
The draws below stay inside these ranges and needn't reach their ends.
There are 2 independent parts, one for each index of `groups`. The reference program is written for one: setup_inputs(seed, part) draws one part's arguments, and reference() takes and returns one part's arrays. A program takes and returns all parts, laid end to end along the dimension named above; an argument that names none is the same for every part. Nothing has to cross between parts.
Inputs may be any that keep to these rules, and one draw needn't show every extreme that they name: `tile_slide`: the 32 tiles of one index of dp include at most 4 tiles of the slides of any one owner; some owner gets exactly 4 from every index of dp; every slide has at least one tile. `slide_owner`: every owner holds exactly 2 slides.
All inputs are finite; a program needn't handle non-finite values.
Results may differ from the reference program's by a relative error of at most 0.0094.
Values may be sent and summed in bfloat16 or wider, within the bound.
No kernel may reach another device: no remote copies, remote signals or barrier semaphores. Data moves between devices by JAX's collectives and lax.ppermute only.
A program may use at most 128 MiB of HBM per device.

```python
import jax
import jax.numpy as jnp
from jax import lax

C = 768
KIN = 3072
POS = 64
A = 384
CLASSES = 2
T_DEV = 32
CAP = 4
SLIDES_DEV = 2
TILES = 512
SLIDES = 32


def route_tables(key):
    owners = SLIDES // SLIDES_DEV
    devices = TILES // T_DEV
    slide_slot = jax.random.permutation(jax.random.fold_in(key, 11), SLIDES)
    owner_of = slide_slot // SLIDES_DEV
    held_slides = jnp.argsort(slide_slot, stable=True)
    hot_owner = jax.random.randint(jax.random.fold_in(key, 12), (), 0, owners)
    device_ids = jnp.arange(devices)
    guard = (hot_owner + 1 + device_ids) % owners
    cand_owner = jnp.arange(owners * CAP) // CAP
    cand_rank = jnp.arange(owners * CAP) % CAP
    priority = jax.random.randint(jax.random.fold_in(key, 13), (devices, owners * CAP), 0, 1 << 20)
    priority = priority * (owners * CAP) + jnp.arange(owners * CAP)[None, :]
    forced = (cand_owner[None, :] == guard[:, None]) & (cand_rank[None, :] < 2) & (device_ids[:, None] < devices - 1)
    priority = jnp.where(forced, cand_rank[None, :] - 2, priority)
    excluded = cand_owner[None, :] == hot_owner
    priority = jnp.where(excluded, (1 << 30) + jnp.arange(owners * CAP)[None, :], priority)
    picks = jnp.argsort(priority, axis=1, stable=True)[:, :T_DEV - CAP]
    all_owner = jnp.concatenate([jnp.full((devices, CAP), hot_owner), cand_owner[picks]], axis=1)
    all_rank = jnp.concatenate([jnp.broadcast_to(jnp.arange(CAP), (devices, CAP)), cand_rank[picks]], axis=1)
    slides_of = held_slides[all_owner * SLIDES_DEV + all_rank % SLIDES_DEV]
    shuffle_key = jax.random.randint(jax.random.fold_in(key, 14), (devices, T_DEV), 0, 1 << 20)
    shuffle_key = shuffle_key * T_DEV + jnp.arange(T_DEV)[None, :]
    shuffle = jnp.argsort(shuffle_key, axis=1, stable=True)
    slides_of = jnp.take_along_axis(slides_of, shuffle, axis=1)
    return (slides_of.reshape(TILES).astype(jnp.int32), owner_of.astype(jnp.int32))


def draw_tile_slide(key, part):
    return route_tables(key)[0]


def draw_slide_owner(key, part):
    return route_tables(key)[1]


def plant(result, rng, low, top_value):
    longest = result.shape.index(max(result.shape))
    spots = []
    for shift in (0, 1):
        where = [jax.random.randint(jax.random.fold_in(rng, axis), (), 0, length) for axis, length in enumerate(result.shape)]
        where[longest] = (where[longest] + shift) % result.shape[longest]
        spots.append(tuple(where))
    return result.at[spots[0]].set(low).at[spots[1]].set(top_value)


def steps_of(own_key, dims, shards, low, top_value):
    gain = 1.0
    for dim, shards_of in shards:
        draws = jax.random.uniform(jax.random.fold_in(jax.random.fold_in(own_key, 6), dim), (shards_of,), jnp.float32, low / len(shards), top_value / len(shards))
        gain = gain * jnp.repeat(jnp.exp(draws), dims[dim] // shards_of).reshape((-1,) + (1,) * (len(dims) - 1 - dim))
    return gain


def bell_draw(rng, dims, scale, most, cuts=(), kind=jnp.bfloat16):
    level = steps_of(rng, dims, cuts, -0.22, 0.18) if cuts else 1.0
    values = jax.random.normal(rng, dims, jnp.float32) * scale * level
    return jnp.minimum(jnp.maximum(values, -most), most).astype(kind)


def setup_inputs(seed: int = 0, part: int = 0) -> dict:
    key_of = jax.random.split(jax.random.key(seed), 10)
    part_keys = jax.random.split(jax.random.fold_in(key_of[9], part), 10)
    tiles = bell_draw(part_keys[0], (TILES, POS, KIN), 1.0, 6.0, ((0, 16),))
    conv_weight = bell_draw(key_of[1], (KIN, C), KIN ** -0.5, 0.109375, ((0, 16),))
    tile_slide = draw_tile_slide(jax.random.fold_in(jax.random.fold_in(key_of[9], part), 71), part)
    slide_owner = draw_slide_owner(jax.random.fold_in(jax.random.fold_in(key_of[9], part), 71), part)
    labels = plant(jax.random.randint(part_keys[4], (SLIDES,), 0, CLASSES), jax.random.fold_in(part_keys[4], 1), 0, CLASSES - 1).astype(jnp.int32)
    attn_v = bell_draw(key_of[5], (C, A), C ** -0.5, 0.21875)
    attn_u = bell_draw(key_of[6], (C, A), C ** -0.5, 0.21875)
    attn_w = jnp.clip(jax.random.uniform(key_of[7], (A,), jnp.float32, -0.5, 0.5), -0.5, 0.5)
    class_w = bell_draw(key_of[8], (C, CLASSES), 0.1, 0.6, (), jnp.float32)
    return dict(tiles=tiles, conv_weight=conv_weight, tile_slide=tile_slide, slide_owner=slide_owner, labels=labels, attn_v=attn_v, attn_u=attn_u, attn_w=attn_w, class_w=class_w)


norm_eps = 1e-05

def encode(pre_act):
    pooled = lax.optimization_barrier(jnp.mean(jnp.maximum(pre_act, 0.0), axis=1))
    centred = pooled - lax.optimization_barrier(jnp.mean(pooled, axis=-1, keepdims=True))
    spread = lax.optimization_barrier(jnp.mean(centred * centred, axis=-1, keepdims=True))
    return centred * lax.rsqrt(spread + norm_eps)

def head(embedded, member, picked, attn_v, attn_u, attn_w, class_w, slide_count):
    highest = lax.Precision.HIGHEST
    contract = (((0,), (0,)), ((), ()))
    act_a = jnp.tanh(jnp.dot(embedded, attn_v, preferred_element_type=jnp.float32))
    act_g = jax.nn.sigmoid(jnp.dot(embedded, attn_u, preferred_element_type=jnp.float32))
    gated_act = act_a * act_g
    tile_score = jnp.dot(gated_act, attn_w, precision=highest)
    live_rows = lax.optimization_barrier(jnp.sum(member, axis=1))
    exp_score = jnp.exp(tile_score) * live_rows
    slide_total = jnp.dot(exp_score, member, precision=highest)
    weight = exp_score * jnp.dot(member, 1.0 / slide_total, precision=highest)
    pool_weight = (member * weight[:, None]).astype(jnp.bfloat16)
    slide_emb = lax.dot_general(pool_weight, embedded, contract, preferred_element_type=jnp.float32)
    logits = jnp.dot(slide_emb, class_w, precision=highest)
    exp_logits = jnp.exp(logits)
    class_sum = lax.optimization_barrier(jnp.sum(exp_logits, axis=1))
    onehot = (picked[:, None] == jnp.arange(class_w.shape[1])[None, :]).astype(jnp.float32)
    loss_sum = jnp.sum(jnp.log(class_sum) - lax.optimization_barrier(jnp.sum(logits * onehot, axis=1))) / slide_count
    d_logits = (exp_logits / class_sum[:, None] - onehot) / slide_count
    d_class = lax.dot_general(slide_emb, d_logits, contract, precision=highest)
    d_slide = jnp.dot(d_logits, class_w.T, precision=highest)
    d_rows = jnp.dot(member, d_slide, precision=highest)
    d_weight = lax.optimization_barrier(jnp.sum(embedded.astype(jnp.float32) * d_rows, axis=1))
    centre = jnp.dot(member, jnp.dot(weight * d_weight, member, precision=highest), precision=highest)
    d_score = weight * (d_weight - centre)
    attn_w_grad = jnp.dot(d_score, gated_act, precision=highest)
    d_gated = d_score[:, None] * attn_w[None, :]
    d_pre_a = (d_gated * act_g * (1.0 - act_a * act_a)).astype(jnp.bfloat16)
    d_pre_g = (d_gated * act_a * act_g * (1.0 - act_g)).astype(jnp.bfloat16)
    attn_v_grad = lax.dot_general(embedded, d_pre_a, contract, preferred_element_type=jnp.float32)
    attn_u_grad = lax.dot_general(embedded, d_pre_g, contract, preferred_element_type=jnp.float32)
    kept_weight = lax.optimization_barrier(jnp.sum(pool_weight.astype(jnp.float32), axis=1))
    d_embedded = kept_weight[:, None] * d_rows
    d_embedded = d_embedded + jnp.dot(d_pre_a, attn_v.T, preferred_element_type=jnp.float32)
    d_embedded = d_embedded + jnp.dot(d_pre_g, attn_u.T, preferred_element_type=jnp.float32)
    return (logits, loss_sum, d_embedded, attn_v_grad, attn_u_grad, attn_w_grad, d_class)

def reference(tiles, conv_weight, tile_slide, slide_owner, labels, attn_v, attn_u, attn_w, class_w):
    tile_rows = tiles.reshape(TILES * POS, KIN)
    pre_act = jnp.dot(tile_rows, conv_weight, preferred_element_type=jnp.float32).reshape(TILES, POS, C)
    embedded, back_fn = jax.vjp(encode, pre_act)
    embedded = embedded.astype(jnp.bfloat16)
    member = (tile_slide[:, None] == jnp.arange(SLIDES)[None, :]).astype(jnp.float32)
    logits, loss_sum, d_embedded, v_grad, u_grad, w_grad, c_grad = head(embedded, member, labels, attn_v, attn_u, attn_w, class_w, SLIDES)
    rounded = lax.optimization_barrier(d_embedded.astype(jnp.bfloat16)).astype(jnp.float32)
    d_pre = back_fn(rounded)[0].astype(jnp.bfloat16).reshape(TILES * POS, C)
    conv_grad = lax.dot_general(tile_rows, d_pre, (((0,), (0,)), ((), ())), preferred_element_type=jnp.float32)
    slide_order = jnp.argsort(slide_owner * SLIDES + jnp.arange(SLIDES), stable=True)
    slide_logits = logits[slide_order]
    return (conv_grad, v_grad, u_grad, w_grad, c_grad, slide_logits, loss_sum.reshape(1))
```

```python
import functools

import jax
import jax.numpy as jnp
from jax import lax
from jax.experimental import pallas as pl
from jax.experimental.pallas import tpu as pltpu
from jax.sharding import PartitionSpec as P

norm_eps = 1e-05
F32 = jnp.float32
BF16 = jnp.bfloat16
LANES = 128
VMEM_LIMIT = 48 * 1024 * 1024


def whole(shape):
    return pl.BlockSpec(shape, lambda *_: (0,) * len(shape))


def forward_kernel(pieces, first, last, positions, where, tiles, *refs):
    ws = refs[:pieces]
    rest = refs[pieces:]
    acc = None
    if not first:
        acc, rest = rest[0], rest[1:]
    if last:
        mask_out, pooled_out, weight = rest
    else:
        acc_out, weight = rest
    share = ws[0].shape[0]

    @pl.when(pl.program_id(0) == 0)
    def _():
        for i in range(pieces):
            start = pl.multiple_of(where[1 + i] * share, share)
            weight[pl.ds(start, share), :] = ws[i][...]

    total = jnp.dot(tiles[...], weight[...], preferred_element_type=F32)
    if not first:
        total = total + acc[...]
    if not last:
        acc_out[...] = total
        return
    mask_out[...] = jnp.where(total > 0, 1.0, jnp.where(total == 0, 0.5, 0.0)).astype(BF16)
    rows, channels = total.shape
    count = rows // positions
    active = jnp.maximum(total, 0.0).reshape(count, positions, channels)
    pooled_out[...] = jnp.sum(active, axis=1) * (1.0 / positions)


def forward_chunk(where, tile_rows, ws, acc, last, positions):
    rows, inputs = tile_rows.shape
    share, channels = ws[0].shape
    pieces = len(ws)
    depth = share * pieces
    block = min(rows, 8 * positions)
    first = acc is None
    tiled = pl.BlockSpec((block, channels), lambda i, w: (i, 0))
    in_specs = [pl.BlockSpec((block, depth), lambda i, w: (i, w[0]))]
    in_specs += [whole((share, channels))] * pieces
    operands = [tile_rows, *ws]
    if not first:
        in_specs.append(tiled)
        operands.append(acc)
    if last:
        out_specs = [tiled, pl.BlockSpec((block // positions, channels), lambda i, w: (i, 0))]
        out_shape = [
            jax.ShapeDtypeStruct((rows, channels), BF16),
            jax.ShapeDtypeStruct((rows // positions, channels), F32),
        ]
    else:
        out_specs = [tiled]
        out_shape = [jax.ShapeDtypeStruct((rows, channels), F32)]
    return pl.pallas_call(
        functools.partial(forward_kernel, pieces, first, last, positions),
        grid_spec=pltpu.PrefetchScalarGridSpec(
            num_scalar_prefetch=1,
            grid=(rows // block,),
            in_specs=in_specs,
            out_specs=out_specs,
            scratch_shapes=[pltpu.VMEM((depth, channels), BF16)],
        ),
        out_shape=out_shape,
        compiler_params=pltpu.CompilerParams(vmem_limit_bytes=VMEM_LIMIT),
        cost_estimate=pl.CostEstimate(
            flops=2 * rows * depth * channels,
            bytes_accessed=2 * rows * depth + 8 * rows * channels,
            transcendentals=0,
        ),
        name="section_forward",
    )(where, *operands)


def member_of(tile_slide, lanes):
    slide = lax.broadcasted_iota(jnp.int32, (tile_slide.shape[0], lanes), 1)
    return (tile_slide == slide).astype(F32)


def normal(pooled):
    centred = pooled - jnp.mean(pooled, axis=-1, keepdims=True)
    spread = jnp.mean(centred * centred, axis=-1, keepdims=True)
    scale = lax.rsqrt(spread + norm_eps)
    return centred * scale, scale


def score_kernel(
    pooled, slide, attn_v, attn_u, attn_w, class_t, emb_out, gated_out, ua_out, ug_out, back_out, stat_out, packet_out
):
    unit, _ = normal(pooled[...])
    emb = unit.astype(BF16)
    emb_out[...] = emb
    act_a = jnp.tanh(jnp.dot(emb, attn_v[...], preferred_element_type=F32))
    act_g = jax.nn.sigmoid(jnp.dot(emb, attn_u[...], preferred_element_type=F32))
    gated = act_a * act_g
    gated_out[...] = gated
    exp_score = jnp.exp(jnp.sum(gated * attn_w[...], axis=1, keepdims=True))
    emb32 = emb.astype(F32)
    classes = class_t.shape[0]
    reads = [jnp.sum(emb32 * class_t[k : k + 1, :], axis=1, keepdims=True) for k in range(classes)]
    lanes = packet_out.shape[1]
    member = member_of(slide[...], lanes)
    total = jnp.sum(member * exp_score, axis=0, keepdims=True)
    own_total = jnp.sum(member * total, axis=1, keepdims=True)
    part = jnp.where(own_total > 0, exp_score / own_total, 0.0)
    packet_out[...] = jnp.zeros_like(packet_out)
    packet_out[0:1, :] = total
    for k in range(classes):
        packet_out[k + 1 : k + 2, :] = jnp.sum(member * (part * reads[k]), axis=0, keepdims=True)
    column = lax.broadcasted_iota(jnp.int32, stat_out.shape, 1)
    stats = jnp.where(column == 0, exp_score, 0.0)
    for k in range(classes):
        stats = jnp.where(column == k + 1, reads[k], stats)
    stat_out[...] = stats
    ua = (attn_w[...] * act_g * (1.0 - act_a * act_a)).astype(BF16)
    ug = (attn_w[...] * act_a * act_g * (1.0 - act_g)).astype(BF16)
    ua_out[...] = ua
    ug_out[...] = ug
    contract = (((1,), (1,)), ((), ()))
    back_out[...] = lax.dot_general(ua, attn_v[...], contract, preferred_element_type=F32) + lax.dot_general(
        ug, attn_u[...], contract, preferred_element_type=F32
    )


def score(pooled, slide, attn_v, attn_u, attn_w, class_t, lanes):
    tiles, channels = pooled.shape
    hidden = attn_v.shape[1]
    return pl.pallas_call(
        score_kernel,
        out_shape=[
            jax.ShapeDtypeStruct((tiles, channels), BF16),
            jax.ShapeDtypeStruct((tiles, hidden), F32),
            jax.ShapeDtypeStruct((tiles, hidden), BF16),
            jax.ShapeDtypeStruct((tiles, hidden), BF16),
            jax.ShapeDtypeStruct((tiles, channels), F32),
            jax.ShapeDtypeStruct((tiles, LANES), F32),
            jax.ShapeDtypeStruct((8, lanes), F32),
        ],
        compiler_params=pltpu.CompilerParams(vmem_limit_bytes=VMEM_LIMIT),
        name="tile_scores",
    )(pooled, slide, attn_v, attn_u, attn_w, class_t)


def merge(one, other):
    total = one[0:1] + other[0:1]
    safe = jnp.where(total > 0, total, 1.0)
    mean = one * (one[0:1] / safe) + other * (other[0:1] / safe)
    row = lax.broadcasted_iota(jnp.int32, one.shape, 0)
    return jnp.where(row == 0, total, mean)


def grads_kernel(
    packets,
    slides,
    shards,
    where,
    *refs,
):
    boxes = refs[:packets]
    (pooled, emb, gated, ua, ug, back, stat, slide, owner, label, class_t) = refs[packets : packets + 11]
    (scale_out, small_out, term_keep, term_send, logit_out, loss_out) = refs[packets + 11 :]
    packet = boxes[0][...]
    for box in boxes[1:]:
        packet = merge(packet, box[...])
    classes = class_t.shape[0]
    lanes = packet.shape[1]
    total = packet[0:1]
    live = lax.broadcasted_iota(jnp.int32, (1, lanes), 1) < slides
    logits = [jnp.where(live, packet[k + 1 : k + 2], 0.0) for k in range(classes)]
    exp_logits = [jnp.exp(v) for v in logits]
    class_sum = functools.reduce(jnp.add, exp_logits)
    hot = [jnp.where(label[...] == k, 1.0, 0.0) for k in range(classes)]
    picked = functools.reduce(jnp.add, [v * h for v, h in zip(logits, hot)])
    loss = jnp.where(live, jnp.log(class_sum) - picked, 0.0)
    loss_out[...] = jnp.broadcast_to(jnp.sum(loss, axis=1, keepdims=True) / slides, loss_out.shape)
    d_logits = [jnp.where(live, (e / class_sum - h) / slides, 0.0) for e, h in zip(exp_logits, hot)]
    centre = functools.reduce(jnp.add, [d * v for d, v in zip(d_logits, logits)])

    mine = jnp.where((owner[...] == where[0]) & live, 1.0, 0.0)
    up = lax.broadcasted_iota(jnp.int32, (lanes, lanes), 0)
    across = lax.broadcasted_iota(jnp.int32, (lanes, lanes), 1)
    rank = jnp.dot(
        jnp.broadcast_to(mine, (8, lanes)), jnp.where(up < across, 1.0, 0.0), preferred_element_type=F32
    )
    wanted = lax.broadcasted_iota(jnp.int32, (8, lanes), 0).astype(F32)
    chosen = jnp.where((rank == wanted) & (mine > 0), 1.0, 0.0)
    column = lax.broadcasted_iota(jnp.int32, (8, LANES), 1)
    rows = jnp.zeros((8, LANES), F32)
    for k in range(classes):
        rows = jnp.where(column == k, jnp.sum(chosen * logits[k], axis=1, keepdims=True), rows)
    logit_out[...] = rows

    member = member_of(slide[...], lanes)

    def of_tile(row):
        return jnp.sum(member * row, axis=1, keepdims=True)

    stats = stat[...]
    weight = stats[:, 0:1] / of_tile(total)
    d_tile = [of_tile(d) for d in d_logits]
    d_weight = functools.reduce(jnp.add, [d * stats[:, k + 1 : k + 2] for k, d in enumerate(d_tile)])
    d_score = weight * (d_weight - of_tile(centre))
    kept = weight.astype(BF16).astype(F32)
    d_rows = functools.reduce(jnp.add, [d * class_t[k : k + 1, :] for k, d in enumerate(d_tile)])
    d_emb = (kept * d_rows + d_score * back[...]).astype(BF16).astype(F32)
    unit, inv = normal(pooled[...])
    d_pool = inv * (
        d_emb
        - jnp.mean(d_emb, axis=-1, keepdims=True)
        - unit * jnp.mean(d_emb * unit, axis=-1, keepdims=True)
    )
    scale_out[...] = d_pool

    emb16 = emb[...]
    emb32 = emb16.astype(F32)
    small_out[...] = jnp.zeros_like(small_out)
    channels = emb16.shape[1]
    for k in range(classes):
        small_out[k : k + 1, :channels] = jnp.sum(emb32 * (kept * d_tile[k]), axis=0, keepdims=True)
    hidden = gated.shape[1]
    small_out[classes : classes + 1, :hidden] = jnp.sum(gated[...] * d_score, axis=0, keepdims=True)

    d_pre_a = (d_score * ua[...].astype(F32)).astype(BF16)
    d_pre_g = (d_score * ug[...].astype(F32)).astype(BF16)
    d_pre = jnp.concatenate([d_pre_a, d_pre_g], axis=1)
    term = lax.dot_general(emb16, d_pre, (((0,), (0,)), ((), ())), preferred_element_type=F32)
    if shards is None:
        term_keep[...] = term
        term_send[...] = jnp.zeros_like(term_send)
        return
    zs, ys, cs = shards
    share = channels // (zs * ys * cs)
    y, c = where[1], where[2]
    for iz in range(zs):
        for iy in range(ys):
            for ic in range(cs):
                at = ((iz * ys + iy) * cs + ic) * share
                block = term[at : at + share]

                @pl.when(c == ic)
                def _():
                    term_keep[y ^ iy, iz] = block

                @pl.when(c != ic)
                def _():
                    term_send[y ^ iy, iz] = block.astype(BF16)


def grads(where, boxes, local, slide, owner, label, class_t, slides, shards):
    pooled, emb, gated, ua, ug, back, stat = local
    tiles, channels = pooled.shape
    hidden = gated.shape[1]
    if shards is None:
        keep_shape, send_shape = (channels, 2 * hidden), (16, LANES)
    else:
        zs, ys, cs = shards
        keep_shape = send_shape = (ys, zs, channels // (zs * ys * cs), 2 * hidden)
    vmem = pl.BlockSpec(memory_space=pltpu.VMEM)
    return pl.pallas_call(
        functools.partial(grads_kernel, len(boxes), slides, shards),
        in_specs=[pl.BlockSpec(memory_space=pltpu.SMEM)] + [vmem] * (len(boxes) + 11),
        out_shape=[
            jax.ShapeDtypeStruct((tiles, channels), F32),
            jax.ShapeDtypeStruct((8, max(channels, hidden)), F32),
            jax.ShapeDtypeStruct(keep_shape, F32),
            jax.ShapeDtypeStruct(send_shape, BF16),
            jax.ShapeDtypeStruct((8, LANES), F32),
            jax.ShapeDtypeStruct((8, LANES), F32),
        ],
        compiler_params=pltpu.CompilerParams(vmem_limit_bytes=VMEM_LIMIT),
        name="head_grads",
    )(where, *boxes, pooled, emb, gated, ua, ug, back, stat, slide, owner, label, class_t)


def spread_kernel(positions, mask, scale, out):
    rows, channels = mask.shape
    count = rows // positions
    scaled = (scale[...] * (1.0 / positions)).astype(BF16)
    masks = mask[...].reshape(count, positions, channels)
    out[...] = (masks * scaled[:, None, :]).reshape(rows, channels)


def spread(mask, scale, positions):
    rows, channels = mask.shape
    block = min(rows, 8 * positions)
    tiled = pl.BlockSpec((block, channels), lambda i: (i, 0))
    return pl.pallas_call(
        functools.partial(spread_kernel, positions),
        grid=(rows // block,),
        in_specs=[tiled, pl.BlockSpec((block // positions, channels), lambda i: (i, 0))],
        out_specs=tiled,
        out_shape=jax.ShapeDtypeStruct((rows, channels), BF16),
        compiler_params=pltpu.CompilerParams(vmem_limit_bytes=VMEM_LIMIT),
        name="section_spread",
    )(mask, scale)


def backward_kernel(ys, cs, where, tiles, d_pre, keep, send):
    term = lax.dot_general(tiles[...], d_pre[...], (((0,), (0,)), ((), ())), preferred_element_type=F32)
    share = term.shape[0] // cs
    c = where[2]
    for ic in range(cs):
        block = term[ic * share : (ic + 1) * share]

        @pl.when(c == ic)
        def _():
            keep[0] = block

        @pl.when(c != ic)
        def _():
            send[0] = block.astype(BF16)


def backward_chunk(where, tile_rows, d_pre, ys, cs, share):
    rows, inputs = tile_rows.shape
    channels = d_pre.shape[1]
    width = cs * share
    out = pl.BlockSpec((1, share, channels), lambda i, w: (i ^ w[1], 0, 0))
    return pl.pallas_call(
        functools.partial(backward_kernel, ys, cs),
        grid_spec=pltpu.PrefetchScalarGridSpec(
            num_scalar_prefetch=1,
            grid=(ys,),
            in_specs=[
                pl.BlockSpec((rows, width), lambda i, w: (0, w[0] * ys + i)),
                whole((rows, channels)),
            ],
            out_specs=[out, out],
        ),
        out_shape=[
            jax.ShapeDtypeStruct((ys, share, channels), F32),
            jax.ShapeDtypeStruct((ys, share, channels), BF16),
        ],
        compiler_params=pltpu.CompilerParams(vmem_limit_bytes=VMEM_LIMIT),
        cost_estimate=pl.CostEstimate(
            flops=2 * rows * width * ys * channels,
            bytes_accessed=2 * rows * width * ys + 2 * rows * channels,
            transcendentals=0,
        ),
        name="section_backward",
    )(where, tile_rows, d_pre)


def grid_of(devices):
    return (4, 2, 2) if devices == 16 else None


def moves(shape):
    zs, ys, cs = shape

    def at(z, y, c):
        return (z * ys + y) * cs + c

    every = [(z, y, c) for z in range(zs) for y in range(ys) for c in range(cs)]
    core = [(at(*i), at(i[0], i[1], i[2] ^ 1)) for i in every]
    row = [(at(*i), at(i[0], i[1] ^ 1, i[2])) for i in every]

    def deep(step):
        return [(at(*i), at((i[0] + step) % zs, i[1], i[2])) for i in every]

    return core, row, deep


def send(x, pairs):
    return lax.ppermute(x, "dp", pairs)


def per_device(tiles, conv_weight, tile_slide, slide_owner, labels, attn_v, attn_u, attn_w, class_w):
    tile_count, positions, inputs = tiles.shape
    share, channels = conv_weight.shape
    hidden = attn_v.shape[1]
    classes = class_w.shape[1]
    slides = slide_owner.shape[0]
    devices = lax.axis_size("dp")
    me = lax.axis_index("dp")
    shape = grid_of(devices)
    rows = tile_count * positions
    tile_rows = tiles.reshape(rows, inputs)
    lanes = -(-slides // LANES) * LANES
    pad = lanes - slides
    slide = tile_slide[:, None]
    owner = jnp.pad(slide_owner, (0, pad), constant_values=-1)[None, :]
    label = jnp.pad(labels, (0, pad), constant_values=-1)[None, :]
    class_t = class_w.T
    attn_w_row = attn_w[None, :]

    if shape is None:
        where = jnp.zeros((2,), jnp.int32)
        gathered = lax.all_gather(conv_weight, "dp", axis=0, tiled=True)
        mask, pooled = forward_chunk(where, tile_rows, [gathered], None, True, positions)
    else:
        zs, ys, cs = shape
        core, row, deep = moves(shape)
        z, y, c = me // (ys * cs), me // cs % ys, me % cs
        place = jnp.stack([y * cs + c, y * cs + (c ^ 1), (y ^ 1) * cs + c, (y ^ 1) * cs + (c ^ 1)])
        mine, acc = conv_weight, None
        for step in range(zs):
            across = send(mine, row)
            pieces = [mine, send(mine, core), across, send(across, core)]
            where = jnp.concatenate([((z - step) % zs)[None], place]).astype(jnp.int32)
            last = step == zs - 1
            out = forward_chunk(where, tile_rows, pieces, acc, last, positions)
            if last:
                mask, pooled = out
            else:
                acc = out[0]
                mine = send(mine, deep(1))

    emb, gated, ua, ug, back, stat, packet = score(pooled, slide, attn_v, attn_u, attn_w_row, class_t, lanes)
    local = (pooled, emb, gated, ua, ug, back, stat)
    if shape is None:
        boxes = lax.all_gather(packet, "dp", axis=0)
        boxes = [boxes[i] for i in range(devices)]
        where = me[None].astype(jnp.int32)
    else:
        packet = merge(packet, send(packet, core))
        packet = merge(packet, send(packet, row))
        boxes = [packet] + [send(packet, deep(i)) for i in (2, 1, 3)]
        where = jnp.stack([me, y, c]).astype(jnp.int32)
    scale, small, term_keep, term_send, logit_rows, loss_rows = grads(
        where, boxes, local, slide, owner, label, class_t, slides, shape
    )
    slides_here = slides // devices
    logits = logit_rows[:slides_here, :classes]
    loss = loss_rows[0, :1]
    total = jnp.sum(lax.all_gather(small, "dp", axis=0), axis=0)
    class_grad = total[:classes, :channels].T
    attn_w_grad = total[classes, :hidden]
    d_pre = spread(mask, scale, positions)

    if shape is None:
        contract = (((0,), (0,)), ((), ()))
        term = lax.dot_general(tile_rows, d_pre, contract, preferred_element_type=F32)
        conv_grad = lax.psum_scatter(term, "dp", scatter_dimension=0, tiled=True)
        pair = lax.psum_scatter(term_keep, "dp", scatter_dimension=0, tiled=True)
        return (conv_grad, pair[:, :hidden], pair[:, hidden:], attn_w_grad, class_grad, logits, loss)

    def chip_sum(keep, away):
        got = send(away, core).astype(F32)
        over = send((keep[1] + got[1]).astype(BF16), row)
        return keep[0] + got[0] + over.astype(F32)

    pair_sum = chip_sum(term_keep, term_send)
    got = [
        send(lax.dynamic_index_in_dim(pair_sum, (z + i) % zs, 0, False).astype(BF16), deep(i)).astype(F32)
        for i in (2, 1, 3)
    ]
    pair = lax.dynamic_index_in_dim(pair_sum, z, 0, False) + got[0] + got[1] + got[2]

    arrived = []
    for step in (2, 1, 3, 0):
        where = jnp.stack([(z + step) % zs, y, c]).astype(jnp.int32)
        keep, away = backward_chunk(where, tile_rows, d_pre, ys, cs, share)
        block = chip_sum(keep, away)
        if step:
            arrived.append(send(block.astype(BF16), deep(step)))
        else:
            conv_grad = block
    for block in arrived:
        conv_grad = conv_grad + block.astype(F32)
    return (conv_grad, pair[:, :hidden], pair[:, hidden:], attn_w_grad, class_grad, logits, loss)


def solution(mesh):
    in_specs = (
        P(("groups", "dp"), None, None),
        P("dp", None),
        P(("groups", "dp")),
        P("groups"),
        P("groups"),
        P(),
        P(),
        P(),
        P(),
    )
    out_specs = (
        P(("groups", "dp"), None),
        P(("groups", "dp"), None),
        P(("groups", "dp"), None),
        P("groups"),
        P("groups", None),
        P(("groups", "dp"), None),
        P("groups"),
    )
    return jax.shard_map(per_device, mesh=mesh, in_specs=in_specs, out_specs=out_specs, check_vma=False)
```

```python
import functools

import jax
import jax.numpy as jnp
from jax import lax
from jax.experimental import pallas as pl
from jax.experimental.pallas import tpu as pltpu
from jax.sharding import PartitionSpec as P

norm_eps = 1e-05
F32 = jnp.float32
BF16 = jnp.bfloat16
LANES = 128
EXTRA = 16
VMEM_LIMIT = 32 * 1024 * 1024


IN_VMEM = pl.BlockSpec(memory_space=pltpu.VMEM)
IN_SMEM = pl.BlockSpec(memory_space=pltpu.SMEM)
IN_HBM = pl.BlockSpec(memory_space=pltpu.HBM)
ANYWHERE = pl.BlockSpec(memory_space=pl.ANY)


def in_hbm(x):
    return pltpu.with_memory_space_constraint(x, pltpu.HBM)


def split_kernel(cs, share, where, tiles, own, away):
    inputs = tiles.shape[1]
    c = where[0]
    for ic in range(cs):
        starts = range(ic * share, inputs, cs * share)
        part = jnp.concatenate([tiles[:, at : at + share] for at in starts], axis=1)

        @pl.when(c == ic)
        def _():
            own[...] = part

        @pl.when(c != ic)
        def _():
            away[...] = part


def split_inputs(c, tile_rows, cs, share, part, parts):
    rows, inputs = tile_rows.shape
    rows = rows // parts
    block = min(rows, 256)
    skip = part * (rows // block)
    half = pl.BlockSpec((block, inputs // cs), lambda i: (i, 0))
    return pl.pallas_call(
        functools.partial(split_kernel, cs, share),
        grid=(rows // block,),
        in_specs=[IN_SMEM, pl.BlockSpec((block, inputs), lambda i: (skip + i, 0))],
        out_specs=[half, half],
        out_shape=[pltpu.HBM((rows, inputs // cs), BF16)] * 2,
        compiler_params=pltpu.CompilerParams(vmem_limit_bytes=VMEM_LIMIT),
        name="split_inputs",
    )(c[None].astype(jnp.int32), tile_rows)


def forward_kernel(groups, pieces, first, last, positions, where, token, tiles, *refs):
    ws = refs[:pieces]
    rest = refs[pieces:]
    if not first:
        acc_in, rest = rest[0], rest[1:]
    if last:
        mask_out, pooled_out, _, weight, rows_in, totals, sems, masks = rest
    else:
        acc_out, _, weight, rows_in, totals, sems = rest
    blocks, block, depth = rows_in.shape
    share = ws[0].shape[0]
    wide = depth // groups

    def here(i):
        return pl.ds(pl.multiple_of(i * block, block), block)

    def fetch(i, g):
        across = pl.ds(pl.multiple_of(where[g] * wide, wide), wide)
        to = rows_in.at[i, :, pl.ds(g * wide, wide)]
        return pltpu.make_async_copy(tiles.at[here(i), across], to, sems.at[3 + g, i])

    def resume(i):
        return pltpu.make_async_copy(acc_in.at[here(i)], totals.at[i], sems.at[1, i])

    def store(i):
        if last:
            return pltpu.make_async_copy(masks.at[i], mask_out.at[here(i)], sems.at[2, i])
        return pltpu.make_async_copy(totals.at[i], acc_out.at[here(i)], sems.at[2, i])

    for i in range(blocks):
        for g in range(groups):
            fetch(i, g).start()
        if not first:
            resume(i).start()
    for i in range(pieces):
        start = pl.multiple_of(where[groups + i] * share, share)
        weight[pl.ds(start, share), :] = ws[i][...]
    count = block // positions

    @pl.loop(0, blocks)
    def _(i):
        for g in range(groups):
            fetch(i, g).wait()
        total = jnp.dot(rows_in[i], weight[...], preferred_element_type=F32)
        if not first:
            resume(i).wait()
            total = total + totals[i]
        if last:
            masks[i] = jnp.where(total > 0, 1.0, jnp.where(total == 0, 0.5, 0.0)).astype(BF16)
            active = jnp.maximum(total, 0.0).reshape(count, positions, total.shape[1])
            pooled_out[pl.ds(pl.multiple_of(i * count, count), count), :] = jnp.sum(active, axis=1) * (1.0 / positions)
        else:
            totals[i] = total
        store(i).start()

    for i in range(blocks):
        store(i).wait()


def forward_chunk(where, token, tile_rows, ws, acc, last, positions, groups=1):
    rows, inputs = tile_rows.shape
    share, channels = ws[0].shape
    pieces = len(ws)
    depth = share * pieces
    block = 8 * positions if rows % (8 * positions) == 0 else rows
    first = acc is None
    in_specs = [IN_SMEM, ANYWHERE, IN_HBM] + [IN_VMEM] * pieces
    operands = [where, token, tile_rows, *ws]
    alias = {}
    if not first:
        in_specs.append(IN_HBM)
        operands.append(in_hbm(acc))
    if last:
        out_shape = [
            pltpu.HBM((rows, channels), BF16),
            jax.ShapeDtypeStruct((rows // positions, channels), F32),
        ]
        out_specs = [IN_HBM, IN_VMEM]
    else:
        out_shape = [pltpu.HBM((rows, channels), F32)]
        out_specs = [IN_HBM]
        if not first:
            alias = {len(operands) - 1: 0}
    alias[1] = len(out_shape)
    out_specs.append(ANYWHERE)
    out_shape.append(jax.ShapeDtypeStruct(token.shape, token.dtype))
    blocks = rows // block
    scratch = [
        pltpu.VMEM((depth, channels), BF16),
        pltpu.VMEM((blocks, block, depth), BF16),
        pltpu.VMEM((blocks, block, channels) if not (first and last) else (1, 8, LANES), F32),
        pltpu.SemaphoreType.DMA((3 + groups, blocks)),
    ]
    if last:
        scratch.append(pltpu.VMEM((blocks, block, channels), BF16))
    return pl.pallas_call(
        functools.partial(forward_kernel, groups, pieces, first, last, positions),
        in_specs=in_specs,
        out_specs=out_specs,
        scratch_shapes=scratch,
        out_shape=out_shape,
        input_output_aliases=alias,
        compiler_params=pltpu.CompilerParams(vmem_limit_bytes=VMEM_LIMIT if depth < inputs else 2 * VMEM_LIMIT - 2**22),
        cost_estimate=pl.CostEstimate(
            flops=2 * rows * depth * channels,
            bytes_accessed=2 * rows * depth,
            transcendentals=0,
        ),
        name="section_forward",
    )(*operands)


def member_of(tile_slide, lanes):
    slide = lax.broadcasted_iota(jnp.int32, (tile_slide.shape[0], lanes), 1)
    return (tile_slide == slide).astype(F32)


def normal(pooled):
    centred = pooled - jnp.mean(pooled, axis=-1, keepdims=True)
    spread = jnp.mean(centred * centred, axis=-1, keepdims=True)
    scale = lax.rsqrt(spread + norm_eps)
    return centred * scale, scale


def score_kernel(pooled, slide, attn_v, attn_u, attn_w, class_t, narrow_out, wide_out, packet_out):
    channels, hidden = attn_v.shape
    unit, _ = normal(pooled[...])
    emb = unit.astype(BF16)
    narrow_out[:, :channels] = emb
    act_a = jnp.tanh(jnp.dot(emb, attn_v[...], preferred_element_type=F32))
    act_g = jax.nn.sigmoid(jnp.dot(emb, attn_u[...], preferred_element_type=F32))
    gated = act_a * act_g
    wide_out[:, :hidden] = gated
    exp_score = jnp.exp(jnp.sum(gated * attn_w[...], axis=1, keepdims=True))
    emb32 = emb.astype(F32)
    classes = class_t.shape[0]
    reads = [jnp.sum(emb32 * class_t[k : k + 1, :], axis=1, keepdims=True) for k in range(classes)]
    lanes = packet_out.shape[1]
    member = member_of(slide[...], lanes)
    total = jnp.sum(member * exp_score, axis=0, keepdims=True)
    own_total = jnp.sum(member * total, axis=1, keepdims=True)
    part = jnp.where(own_total > 0, exp_score / own_total, 0.0)
    packet_out[...] = jnp.zeros_like(packet_out)
    packet_out[0:1, :] = total
    for k in range(classes):
        packet_out[k + 1 : k + 2, :] = jnp.sum(member * (part * reads[k]), axis=0, keepdims=True)
    column = lax.broadcasted_iota(jnp.int32, (emb.shape[0], LANES), 1)
    stats = jnp.where(column == 0, exp_score, 0.0)
    for k in range(classes):
        stats = jnp.where(column == k + 1, reads[k], stats)
    wide_out[:, hidden : hidden + LANES] = jnp.where(column == classes + 1, slide[...].astype(F32), stats)
    ua = (attn_w[...] * act_g * (1.0 - act_a * act_a)).astype(BF16)
    ug = (attn_w[...] * act_a * act_g * (1.0 - act_g)).astype(BF16)
    narrow_out[:, channels : channels + hidden] = ua
    narrow_out[:, channels + hidden :] = ug
    contract = (((1,), (1,)), ((), ()))
    wide_out[:, hidden + LANES : hidden + LANES + channels] = pooled[...]
    wide_out[:, hidden + LANES + channels :] = lax.dot_general(ua, attn_v[...], contract, preferred_element_type=F32) + lax.dot_general(
        ug, attn_u[...], contract, preferred_element_type=F32
    )


def score(pooled, slide, attn_v, attn_u, attn_w, class_t, lanes):
    tiles, channels = pooled.shape
    hidden = attn_v.shape[1]
    return pl.pallas_call(
        score_kernel,
        out_shape=[
            jax.ShapeDtypeStruct((tiles, channels + 2 * hidden), BF16),
            jax.ShapeDtypeStruct((tiles, hidden + LANES + 2 * channels), F32),
            jax.ShapeDtypeStruct((8, lanes), F32),
        ],
        compiler_params=pltpu.CompilerParams(vmem_limit_bytes=VMEM_LIMIT),
        name="tile_scores",
    )(pooled, slide, attn_v, attn_u, attn_w, class_t)


def merge(one, other):
    total = one[0:1] + other[0:1]
    safe = jnp.where(total > 0, total, 1.0)
    mean = one * (one[0:1] / safe) + other * (other[0:1] / safe)
    row = lax.broadcasted_iota(jnp.int32, one.shape, 0)
    return jnp.where(row == 0, total, mean)


def grads_kernel(
    packets,
    slides,
    shards,
    sides,
    positions,
    where,
    *refs,
):
    inputs, refs = refs[:sides], refs[sides:]
    boxes = refs[:packets]
    refs = refs[packets:]
    narrows, wides, refs = refs[:sides], refs[sides : 2 * sides], refs[2 * sides :]
    (owner, label, class_t, d_pre_out, term_keep, term_send, logit_out, loss_out, masks, sems) = refs
    blocks, block, channels = masks.shape
    per_side = blocks // sides
    fetches = [
        pltpu.make_async_copy(
            inputs[i // per_side].at[pl.ds(i % per_side * block, block)], masks.at[i], sems.at[i]
        )
        for i in range(blocks)
    ]
    for fetch in fetches:
        fetch.start()
    packet = boxes[0][...]
    for box in boxes[1:]:
        packet = merge(packet, box[...])
    classes = class_t.shape[0]
    lanes = packet.shape[1]
    total = packet[0:1]
    live = lax.broadcasted_iota(jnp.int32, (1, lanes), 1) < slides
    logits = [jnp.where(live, packet[k + 1 : k + 2], 0.0) for k in range(classes)]
    exp_logits = [jnp.exp(v) for v in logits]
    class_sum = functools.reduce(jnp.add, exp_logits)
    hot = [jnp.where(label[...] == k, 1.0, 0.0) for k in range(classes)]
    picked = functools.reduce(jnp.add, [v * h for v, h in zip(logits, hot)])
    loss = jnp.where(live, jnp.log(class_sum) - picked, 0.0)
    loss_out[...] = jnp.broadcast_to(jnp.sum(loss, axis=1, keepdims=True) / slides, loss_out.shape)
    d_logits = [jnp.where(live, (e / class_sum - h) / slides, 0.0) for e, h in zip(exp_logits, hot)]
    centre = functools.reduce(jnp.add, [d * v for d, v in zip(d_logits, logits)])

    mine = jnp.where((owner[...] == where[0]) & live, 1.0, 0.0)
    up = lax.broadcasted_iota(jnp.int32, (lanes, lanes), 0)
    across = lax.broadcasted_iota(jnp.int32, (lanes, lanes), 1)
    rank = jnp.dot(
        jnp.broadcast_to(mine, (8, lanes)), jnp.where(up < across, 1.0, 0.0), preferred_element_type=F32
    )
    wanted = lax.broadcasted_iota(jnp.int32, (8, lanes), 0).astype(F32)
    chosen = jnp.where((rank == wanted) & (mine > 0), 1.0, 0.0)
    column = lax.broadcasted_iota(jnp.int32, (8, LANES), 1)
    rows = jnp.zeros((8, LANES), F32)
    for k in range(classes):
        rows = jnp.where(column == k, jnp.sum(chosen * logits[k], axis=1, keepdims=True), rows)
    logit_out[...] = rows

    hidden = wides[0].shape[1] - LANES - 2 * channels

    def tile_terms(wide):
        stats = wide[:, hidden : hidden + LANES]
        member = member_of(stats[:, classes + 1 : classes + 2].astype(jnp.int32), lanes)

        def of_tile(row):
            return jnp.sum(member * row, axis=1, keepdims=True)

        weight = stats[:, 0:1] / of_tile(total)
        d_tile = [of_tile(d) for d in d_logits]
        d_weight = functools.reduce(jnp.add, [d * stats[:, k + 1 : k + 2] for k, d in enumerate(d_tile)])
        return weight.astype(BF16).astype(F32), d_tile, weight * (d_weight - of_tile(centre))

    terms = [tile_terms(wide) for wide in wides]
    count = block // positions
    for side in range(sides):
        kept, d_tile, d_score = terms[side]
        d_rows = functools.reduce(jnp.add, [d * class_t[k : k + 1, :] for k, d in enumerate(d_tile)])
        back = wides[side][:, hidden + LANES + channels :]
        d_emb = (kept * d_rows + d_score * back).astype(BF16).astype(F32)
        unit, inv = normal(wides[side][:, hidden + LANES : hidden + LANES + channels])
        d_pool = inv * (
            d_emb
            - jnp.mean(d_emb, axis=-1, keepdims=True)
            - unit * jnp.mean(d_emb * unit, axis=-1, keepdims=True)
        )
        scaled = (d_pool * (1.0 / positions)).astype(BF16)
        for j in range(per_side):
            i = side * per_side + j
            fetches[i].wait()
            here = masks[i].reshape(count, positions, channels)
            mine = scaled[j * count : (j + 1) * count]
            d_pre_out[i * block : (i + 1) * block] = (here * mine[:, None, :]).reshape(block, channels)

    smalls = [0.0] * classes
    wide_sum = 0.0
    embs, d_pres = [], []
    for (kept, d_tile, d_score), narrow, wide in zip(terms, narrows, wides):
        emb = narrow[:, :channels]
        emb32 = emb.astype(F32)
        for k in range(classes):
            smalls[k] = smalls[k] + jnp.sum(emb32 * (kept * d_tile[k]), axis=0, keepdims=True)
        wide_sum = wide_sum + jnp.sum(wide[:, :hidden] * d_score, axis=0, keepdims=True)
        embs.append(emb)
        d_pres.append((d_score * narrow[:, channels:].astype(F32)).astype(BF16))
    smalls.append(jnp.concatenate([wide_sum, jnp.zeros((1, hidden), F32)], axis=1))
    emb16 = jnp.concatenate(embs, axis=0)
    d_pre = jnp.concatenate(d_pres, axis=0)
    term = lax.dot_general(emb16, d_pre, (((0,), (0,)), ((), ())), preferred_element_type=F32)
    zs, ys, cs = shards
    share = channels // (zs * ys * cs)
    y, c = where[1], where[2]
    small = jnp.concatenate(smalls + [jnp.zeros((EXTRA - len(smalls), 2 * hidden), F32)], axis=0)
    if sides == 1:
        term_keep[:channels] = term
        term_keep[channels:] = small
        term_send[...] = jnp.zeros_like(term_send)
        return
    base = zs * share
    term_keep[base:] = small
    term_send[base:] = halves(small, len(smalls))
    for iy in range(ys):
        for ic in range(cs):
            starts = [((iz * ys + iy) * cs + ic) * share for iz in range(zs)]
            rows = jnp.concatenate([term[at : at + share] for at in starts], axis=0)

            @pl.when((c == ic) & (y == iy))
            def _():
                term_keep[:base] = rows

            @pl.when((c == ic) & (y != iy))
            def _():
                term_send[:base] = rows.astype(BF16)


def halves(small, count):
    high = small.astype(BF16).astype(F32)
    low = small - high
    return jnp.concatenate([high[:count], low[:count], jnp.zeros_like(small[2 * count :])], axis=0).astype(BF16)


def joined(rows, count):
    wide = rows.astype(F32)
    return jnp.concatenate([wide[:count] + wide[count : 2 * count], jnp.zeros_like(wide[count:])], axis=0)


def deep_kernel(count, steps, where, keep, got, own, *away):
    share = own.shape[0] - EXTRA
    zs = len(steps) + 1
    small = keep[zs * share :] + joined(got[zs * share :], count)
    split = halves(small, count)
    for step, out in zip((0, *steps), (own, *away)):
        at = pl.ds(pl.multiple_of((where[0] + step) % zs * share, share), share)
        block = keep[at, :] + got[at, :].astype(F32)
        out[:share] = block.astype(out.dtype)
        out[share:] = small if step == 0 else split


def deep_fold(where, keep, got, steps, count):
    zs = len(steps) + 1
    shape = ((keep.shape[0] - EXTRA) // zs + EXTRA, keep.shape[1])
    return pl.pallas_call(
        functools.partial(deep_kernel, count, steps),
        in_specs=[pl.BlockSpec(memory_space=pltpu.SMEM)] + [pl.BlockSpec(memory_space=pltpu.VMEM)] * 2,
        out_shape=[jax.ShapeDtypeStruct(shape, F32)] + [jax.ShapeDtypeStruct(shape, BF16)] * len(steps),
        compiler_params=pltpu.CompilerParams(vmem_limit_bytes=VMEM_LIMIT),
        name="attention_deep",
    )(where, keep, got)


def last_kernel(count, own, *rest):
    got, (v_out, u_out, small_out) = rest[:-3], rest[-3:]
    share, hidden = v_out.shape
    block = own[:share]
    small = own[share:]
    for one in got:
        block = block + one[:share].astype(F32)
        small = small + joined(one[share:], count)
    v_out[...] = block[:, :hidden]
    u_out[...] = block[:, hidden:]
    small_out[...] = small


def last_fold(own, got, count):
    share, hidden = own.shape[0] - EXTRA, own.shape[1] // 2
    return pl.pallas_call(
        functools.partial(last_kernel, count),
        out_shape=[
            jax.ShapeDtypeStruct((share, hidden), F32),
            jax.ShapeDtypeStruct((share, hidden), F32),
            jax.ShapeDtypeStruct((EXTRA, own.shape[1]), F32),
        ],
        compiler_params=pltpu.CompilerParams(vmem_limit_bytes=VMEM_LIMIT),
        name="attention_last",
    )(own, *got)


def grads(where, masks, boxes, narrows, wides, owner, label, class_t, slides, shards, positions):
    rows, channels = masks[0].shape
    hidden = wides[0].shape[1] - LANES - 2 * channels
    zs, ys, cs = shards
    sides = len(narrows)
    keep_shape = (channels // (ys * cs) + EXTRA, 2 * hidden)
    send_shape = keep_shape if sides > 1 else (16, LANES)
    block = 8 * positions if rows % (8 * positions) == 0 else rows
    operands = [where, *map(in_hbm, masks), *boxes, *narrows, *wides, owner, label, class_t]
    return pl.pallas_call(
        functools.partial(grads_kernel, len(boxes), slides, shards, sides, positions),
        in_specs=[IN_SMEM] + [IN_HBM] * sides + [IN_VMEM] * (len(operands) - 1 - sides),
        out_shape=[
            pltpu.VMEM((sides * rows, channels), BF16) if sides > 1 else jax.ShapeDtypeStruct((rows, channels), BF16),
            jax.ShapeDtypeStruct(keep_shape, F32),
            jax.ShapeDtypeStruct(send_shape, BF16),
            jax.ShapeDtypeStruct((8, LANES), F32),
            jax.ShapeDtypeStruct((8, LANES), F32),
        ],
        scratch_shapes=[
            pltpu.VMEM((sides * rows // block, block, channels), BF16),
            pltpu.SemaphoreType.DMA((sides * rows // block,)),
        ],
        compiler_params=pltpu.CompilerParams(vmem_limit_bytes=VMEM_LIMIT),
        name="head_grads",
    )(*operands)


def backward_kernel(ys, parts, where, token, d_pre, *refs):
    tiles, refs = refs[:parts], refs[parts:]
    near, over, _, refs = refs[0], refs[1], refs[2], refs[3:]
    _, columns, sems = refs
    sides, rows, width = columns.shape
    share = width // ys
    y = where[1]
    across = pl.ds(pl.multiple_of(where[0] * width, width), width)
    fetches = [pltpu.make_async_copy(tiles[i].at[:, across], columns.at[i], sems.at[i]) for i in range(sides)]
    for fetch in fetches:
        fetch.start()
    contract = (((0,), (0,)), ((), ()))
    term = 0.0
    for i in range(0, sides, 2):
        fetches[i].wait()
        fetches[i + 1].wait()
        both = columns[i : i + 2].reshape(2 * rows, width)
        term = term + lax.dot_general(
            both, d_pre[i * rows : (i + 2) * rows], contract, preferred_element_type=F32
        )
    for iy in range(ys):
        block = term[iy * share : (iy + 1) * share]

        @pl.when(y == iy)
        def _():
            near[...] = block

        @pl.when(y != iy)
        def _():
            over[...] = block.astype(BF16)


def backward_chunk(where, token, tiles, d_pre, ys, share):
    rows = tiles[0].shape[0]
    channels = d_pre.shape[1]
    width = ys * share
    operands = [where, token, pltpu.with_memory_space_constraint(d_pre, pltpu.VMEM), *map(in_hbm, tiles)]
    return pl.pallas_call(
        functools.partial(backward_kernel, ys, len(tiles)),
        in_specs=[IN_SMEM, ANYWHERE, IN_VMEM] + [IN_HBM] * len(tiles),
        out_specs=[IN_VMEM, IN_VMEM, IN_VMEM, ANYWHERE],
        scratch_shapes=[
            pltpu.VMEM((len(tiles), rows, width), BF16),
            pltpu.SemaphoreType.DMA((len(tiles),)),
        ],
        out_shape=[
            jax.ShapeDtypeStruct((share, channels), F32),
            jax.ShapeDtypeStruct((share, channels), BF16),
            pltpu.VMEM(d_pre.shape, d_pre.dtype),
            jax.ShapeDtypeStruct(token.shape, token.dtype),
        ],
        input_output_aliases={1: 3, 2: 2},
        compiler_params=pltpu.CompilerParams(vmem_limit_bytes=VMEM_LIMIT),
        cost_estimate=pl.CostEstimate(
            flops=2 * len(tiles) * rows * width * channels,
            bytes_accessed=2 * len(tiles) * rows * width,
            transcendentals=0,
        ),
        name="section_backward",
    )(*operands)


def sum_fold(near, got, dtype):
    total = near
    for one in got:
        total = total + one.astype(F32)
    return total.astype(dtype)


def grid_of(devices):
    return (4, 2, 2) if devices == 16 else None


def moves(shape):
    zs, ys, cs = shape

    def at(z, y, c):
        return (z * ys + y) * cs + c

    every = [(z, y, c) for z in range(zs) for y in range(ys) for c in range(cs)]
    core = [(at(*i), at(i[0], i[1], i[2] ^ 1)) for i in every]
    row = [(at(*i), at(i[0], i[1] ^ 1, i[2])) for i in every]

    def deep(step):
        return [(at(*i), at((i[0] + step) % zs, i[1], i[2])) for i in every]

    return core, row, deep


def together(*values):
    return lax.optimization_barrier(values)


def send(x, pairs):
    return lax.ppermute(x, "dp", pairs)


def per_device(tiles, conv_weight, tile_slide, slide_owner, labels, attn_v, attn_u, attn_w, class_w):
    tile_count, positions, inputs = tiles.shape
    share, channels = conv_weight.shape
    hidden = attn_v.shape[1]
    classes = class_w.shape[1]
    slides = slide_owner.shape[0]
    devices = lax.axis_size("dp")
    me = lax.axis_index("dp")
    shape = grid_of(devices)
    rows = tile_count * positions
    plain_rows = tiles.reshape(rows, inputs)
    tile_rows = in_hbm(plain_rows)
    lanes = -(-slides // LANES) * LANES
    pad = lanes - slides
    slide = tile_slide[:, None]
    owner = jnp.pad(slide_owner, (0, pad), constant_values=-1)[None, :]
    label = jnp.pad(labels, (0, pad), constant_values=-1)[None, :]
    class_t = class_w.T
    attn_w_row = attn_w[None, :]

    token = jnp.zeros((8, LANES), F32)
    if shape is None:
        where = jnp.zeros((2,), jnp.int32)
        gathered = lax.all_gather(conv_weight, "dp", axis=0, tiled=True)
        mask, pooled, token = forward_chunk(where, token, tile_rows, [gathered], None, True, positions)
    else:
        zs, ys, cs = shape
        core, row, deep = moves(shape)
        z, y, c = me // (ys * cs), me // cs % ys, me % cs
        place = [y * cs + c, y * cs + (c ^ 1), (y ^ 1) * cs + c, (y ^ 1) * cs + (c ^ 1)]
        own_parts, away_parts = [], []
        acc, mine = None, conv_weight
        across = send(mine, row)
        waiting, groups, last = [], [], zs - 1
        for step in range(zs):
            if step < last:
                ahead = send(mine, deep(1))
                if step < 2:
                    own_part, away_part = split_inputs(c, tile_rows, cs, share, step, 2)
                    across, ahead, token, own_part, away_part = together(across, ahead, token, own_part, away_part)
                    own_parts.append(own_part)
                    away_parts.append(send(away_part, core))
                else:
                    across, ahead, token, away_parts[0] = together(across, ahead, token, away_parts[0])
                ahead_across = send(ahead, row)
            waiting += [mine, send(mine, core), across, send(across, core)]
            groups.append((z - step) % zs)
            if step > 0:
                spots = [i * ys * cs + at for i in range(len(groups)) for at in place]
                where = jnp.stack([*groups, *spots]).astype(jnp.int32)
                *out, token = forward_chunk(
                    where, token, tile_rows, waiting, acc, step == last, positions, len(groups)
                )
                acc = out[0]
                waiting, groups = [], []
            if step < last:
                mine, across = ahead, ahead_across
            if step == last - 1:
                across, token, away_parts[1] = together(across, token, away_parts[1])
        mask, pooled = out

    narrow, wide, packet = score(pooled, slide, attn_v, attn_u, attn_w_row, class_t, lanes)
    narrows, wides, masks = [narrow], [wide], [mask]
    if shape is None:
        boxes = lax.all_gather(packet, "dp", axis=0)
        boxes = [boxes[i] for i in range(devices)]
        where = jnp.stack([me, me, me]).astype(jnp.int32)
    else:
        packet = merge(packet, send(packet, core))
        packet = merge(packet, send(packet, row))
        packet, *ours = together(packet, narrow, wide, mask)
        for group, one in zip((narrows, wides, masks), ours):
            group[0] = one
            group.append(send(one, core))
        boxes = [packet] + [send(packet, deep(i)) for i in (2, 1, 3)]
        where = jnp.stack([me, y, c]).astype(jnp.int32)
    d_pre, term_keep, term_send, logit_rows, loss_rows = grads(
        where, masks, boxes, narrows, wides, owner, label, class_t, slides, shape or (1, 1, 1), positions
    )
    slides_here = slides // devices
    logits = logit_rows[:slides_here, :classes]
    loss = loss_rows[0, :1]

    if shape is None:
        contract = (((0,), (0,)), ((), ()))
        term = lax.dot_general(plain_rows, d_pre, contract, preferred_element_type=F32)
        conv_grad = lax.psum_scatter(term, "dp", scatter_dimension=0, tiled=True)
        pair = lax.psum_scatter(term_keep[:channels], "dp", scatter_dimension=0, tiled=True)
        small = jnp.sum(lax.all_gather(term_keep[channels:], "dp", axis=0), axis=0)
        return (conv_grad, pair[:, :hidden], pair[:, hidden:], small[classes, :hidden], small[:classes].T, logits, loss)

    extra = classes + 1
    steps = (2, 1, 3)
    term_send, token = together(term_send, token)
    attn_got = send(term_send, row)

    where = {step: jnp.stack([(z + step) % zs, y, c]).astype(jnp.int32) for step in (0, *steps)}
    first, second, third = steps

    parts = own_parts + away_parts

    def chunk(step, d_pre, token):
        return backward_chunk(where[step], token, parts, d_pre, ys, share)

    near_first, over_first, d_pre, token = chunk(first, d_pre, token)
    over_first, attn_got, token = together(over_first, attn_got, token)
    y_first = send(over_first, row)
    own, *away = deep_fold(z[None], term_keep, attn_got, steps, extra)
    *away, token = together(*away, token)
    attn = [send(block, deep(i)) for i, block in zip(steps, away)]
    near_second, over_second, d_pre, token = chunk(second, d_pre, token)
    over_second, y_first, token, *attn = together(over_second, y_first, token, *attn)
    y_second = send(over_second, row)
    out_first, token = together(sum_fold(near_first, [y_first], BF16), token)
    z_first = send(out_first, deep(first))
    near_third, over_third, d_pre, token = chunk(third, d_pre, token)
    over_third, y_second, token = together(over_third, y_second, token)
    y_third = send(over_third, row)
    out_second, token = together(sum_fold(near_second, [y_second], BF16), token)
    z_second = send(out_second, deep(second))
    near_own, over_own, d_pre, token = chunk(0, d_pre, token)
    over_own, y_third, z_first, token = together(over_own, y_third, z_first, token)
    y_own = send(over_own, row)
    out_third, z_second = together(sum_fold(near_third, [y_third], BF16), z_second)
    z_third = send(out_third, deep(third))
    v_grad, u_grad, small = last_fold(own, attn, extra)
    conv_grad = sum_fold(near_own, [y_own, z_first, z_second, z_third], F32)
    return (conv_grad, v_grad, u_grad, small[classes, :hidden], small[:classes].T, logits, loss)


def solution(mesh):
    in_specs = (
        P(("groups", "dp"), None, None),
        P("dp", None),
        P(("groups", "dp")),
        P("groups"),
        P("groups"),
        P(),
        P(),
        P(),
        P(),
    )
    out_specs = (
        P(("groups", "dp"), None),
        P(("groups", "dp"), None),
        P(("groups", "dp"), None),
        P("groups"),
        P("groups", None),
        P(("groups", "dp"), None),
        P("groups"),
    )
    return jax.shard_map(per_device, mesh=mesh, in_specs=in_specs, out_specs=out_specs, check_vma=False)
```

```python
import functools

import jax
import jax.numpy as jnp
from jax import lax
from jax.experimental import pallas as pl
from jax.experimental.pallas import tpu as pltpu
from jax.sharding import PartitionSpec as P

norm_eps = 1e-05
F32 = jnp.float32
BF16 = jnp.bfloat16
LANES = 128
EXTRA = 16
VMEM_LIMIT = 32 * 1024 * 1024


IN_VMEM = pl.BlockSpec(memory_space=pltpu.VMEM)
IN_SMEM = pl.BlockSpec(memory_space=pltpu.SMEM)
IN_HBM = pl.BlockSpec(memory_space=pltpu.HBM)
ANYWHERE = pl.BlockSpec(memory_space=pl.ANY)


def in_hbm(x):
    return pltpu.with_memory_space_constraint(x, pltpu.HBM)


def split_kernel(cs, share, where, tiles, own, away):
    inputs = tiles.shape[1]
    c = where[0]
    for ic in range(cs):
        starts = range(ic * share, inputs, cs * share)
        part = jnp.concatenate([tiles[:, at : at + share] for at in starts], axis=1)

        @pl.when(c == ic)
        def _():
            own[...] = part

        @pl.when(c != ic)
        def _():
            away[...] = part


def split_inputs(c, tile_rows, cs, share, part, parts):
    rows, inputs = tile_rows.shape
    rows = rows // parts
    block = min(rows, 256)
    skip = part * (rows // block)
    half = pl.BlockSpec((block, inputs // cs), lambda i: (i, 0))
    return pl.pallas_call(
        functools.partial(split_kernel, cs, share),
        grid=(rows // block,),
        in_specs=[IN_SMEM, pl.BlockSpec((block, inputs), lambda i: (skip + i, 0))],
        out_specs=[half, half],
        out_shape=[pltpu.HBM((rows, inputs // cs), BF16)] * 2,
        compiler_params=pltpu.CompilerParams(vmem_limit_bytes=VMEM_LIMIT),
        name="split_inputs",
    )(c[None].astype(jnp.int32), tile_rows)


def forward_kernel(groups, pieces, first, last, positions, where, token, tiles, *refs):
    ws = refs[:pieces]
    rest = refs[pieces:]
    if not first:
        acc_in, rest = rest[0], rest[1:]
    if last:
        mask_out, pooled_out, _, weight, rows_in, totals, sems, loads, masks = rest
    else:
        acc_out, _, weight, rows_in, totals, sems, loads = rest
    blocks, block, depth = rows_in.shape
    share = ws[0].shape[0]
    wide = depth // groups

    def here(i):
        return pl.ds(pl.multiple_of(i * block, block), block)

    def fetch(i, g):
        across = pl.ds(pl.multiple_of(where[g] * wide, wide), wide)
        to = rows_in.at[i, :, pl.ds(g * wide, wide)]
        return pltpu.make_async_copy(tiles.at[here(i), across], to, sems.at[3 + g, i])

    def load(i):
        start = pl.multiple_of(where[groups + i] * share, share)
        return pltpu.make_async_copy(ws[i], weight.at[pl.ds(start, share)], loads.at[i])

    def resume(i):
        return pltpu.make_async_copy(acc_in.at[here(i)], totals.at[i], sems.at[1, i])

    def store(i):
        if last:
            return pltpu.make_async_copy(masks.at[i], mask_out.at[here(i)], sems.at[2, i])
        return pltpu.make_async_copy(totals.at[i], acc_out.at[here(i)], sems.at[2, i])

    for i in range(blocks):
        for g in range(groups):
            fetch(i, g).start()
        if not first:
            resume(i).start()
    for i in range(pieces):
        load(i).start()
    for i in range(pieces):
        load(i).wait()
    count = block // positions

    @pl.loop(0, blocks)
    def _(i):
        for g in range(groups):
            fetch(i, g).wait()
        total = jnp.dot(rows_in[i], weight[...], preferred_element_type=F32)
        if not first:
            resume(i).wait()
            total = total + totals[i]
        if last:
            masks[i] = jnp.where(total > 0, 1.0, jnp.where(total == 0, 0.5, 0.0)).astype(BF16)
            active = jnp.maximum(total, 0.0).reshape(count, positions, total.shape[1])
            pooled_out[pl.ds(pl.multiple_of(i * count, count), count), :] = jnp.sum(active, axis=1) * (1.0 / positions)
        else:
            totals[i] = total
        store(i).start()

    for i in range(blocks):
        store(i).wait()


def forward_chunk(where, token, tile_rows, ws, acc, last, positions, groups=1):
    rows, inputs = tile_rows.shape
    share, channels = ws[0].shape
    pieces = len(ws)
    depth = share * pieces
    block = 8 * positions if rows % (8 * positions) == 0 else rows
    first = acc is None
    in_specs = [IN_SMEM, ANYWHERE, IN_HBM] + [ANYWHERE] * pieces
    operands = [where, token, tile_rows, *ws]
    alias = {}
    if not first:
        in_specs.append(IN_HBM)
        operands.append(in_hbm(acc))
    if last:
        out_shape = [
            pltpu.HBM((rows, channels), BF16),
            jax.ShapeDtypeStruct((rows // positions, channels), F32),
        ]
        out_specs = [IN_HBM, IN_VMEM]
    else:
        out_shape = [pltpu.HBM((rows, channels), F32)]
        out_specs = [IN_HBM]
        if not first:
            alias = {len(operands) - 1: 0}
    alias[1] = len(out_shape)
    out_specs.append(ANYWHERE)
    out_shape.append(jax.ShapeDtypeStruct(token.shape, token.dtype))
    blocks = rows // block
    scratch = [
        pltpu.VMEM((depth, channels), BF16),
        pltpu.VMEM((blocks, block, depth), BF16),
        pltpu.VMEM((blocks, block, channels) if not (first and last) else (1, 8, LANES), F32),
        pltpu.SemaphoreType.DMA((3 + groups, blocks)),
        pltpu.SemaphoreType.DMA((pieces,)),
    ]
    if last:
        scratch.append(pltpu.VMEM((blocks, block, channels), BF16))
    return pl.pallas_call(
        functools.partial(forward_kernel, groups, pieces, first, last, positions),
        in_specs=in_specs,
        out_specs=out_specs,
        scratch_shapes=scratch,
        out_shape=out_shape,
        input_output_aliases=alias,
        compiler_params=pltpu.CompilerParams(vmem_limit_bytes=VMEM_LIMIT if depth < inputs else 2 * VMEM_LIMIT - 2**22),
        cost_estimate=pl.CostEstimate(
            flops=2 * rows * depth * channels,
            bytes_accessed=2 * rows * depth,
            transcendentals=0,
        ),
        name="section_forward",
    )(*operands)


def member_of(tile_slide, lanes):
    slide = lax.broadcasted_iota(jnp.int32, (tile_slide.shape[0], lanes), 1)
    return (tile_slide == slide).astype(F32)


def normal(pooled):
    centred = pooled - jnp.mean(pooled, axis=-1, keepdims=True)
    spread = jnp.mean(centred * centred, axis=-1, keepdims=True)
    scale = lax.rsqrt(spread + norm_eps)
    return centred * scale, scale


def score_kernel(pooled, slide, attn_v, attn_u, attn_w, class_t, narrow_out, wide_out, packet_out):
    channels, hidden = attn_v.shape
    unit, _ = normal(pooled[...])
    emb = unit.astype(BF16)
    narrow_out[:, :channels] = emb
    act_a = jnp.tanh(jnp.dot(emb, attn_v[...], preferred_element_type=F32))
    act_g = jax.nn.sigmoid(jnp.dot(emb, attn_u[...], preferred_element_type=F32))
    gated = act_a * act_g
    wide_out[:, :hidden] = gated
    exp_score = jnp.exp(jnp.sum(gated * attn_w[...], axis=1, keepdims=True))
    emb32 = emb.astype(F32)
    classes = class_t.shape[0]
    reads = [jnp.sum(emb32 * class_t[k : k + 1, :], axis=1, keepdims=True) for k in range(classes)]
    lanes = packet_out.shape[1]
    member = member_of(slide[...], lanes)
    total = jnp.sum(member * exp_score, axis=0, keepdims=True)
    own_total = jnp.sum(member * total, axis=1, keepdims=True)
    part = jnp.where(own_total > 0, exp_score / own_total, 0.0)
    packet_out[...] = jnp.zeros_like(packet_out)
    packet_out[0:1, :] = total
    for k in range(classes):
        packet_out[k + 1 : k + 2, :] = jnp.sum(member * (part * reads[k]), axis=0, keepdims=True)
    column = lax.broadcasted_iota(jnp.int32, (emb.shape[0], LANES), 1)
    stats = jnp.where(column == 0, exp_score, 0.0)
    for k in range(classes):
        stats = jnp.where(column == k + 1, reads[k], stats)
    wide_out[:, hidden : hidden + LANES] = jnp.where(column == classes + 1, slide[...].astype(F32), stats)
    ua = (attn_w[...] * act_g * (1.0 - act_a * act_a)).astype(BF16)
    ug = (attn_w[...] * act_a * act_g * (1.0 - act_g)).astype(BF16)
    narrow_out[:, channels : channels + hidden] = ua
    narrow_out[:, channels + hidden :] = ug
    contract = (((1,), (1,)), ((), ()))
    wide_out[:, hidden + LANES : hidden + LANES + channels] = pooled[...]
    wide_out[:, hidden + LANES + channels :] = lax.dot_general(ua, attn_v[...], contract, preferred_element_type=F32) + lax.dot_general(
        ug, attn_u[...], contract, preferred_element_type=F32
    )


def score(pooled, slide, attn_v, attn_u, attn_w, class_t, lanes):
    tiles, channels = pooled.shape
    hidden = attn_v.shape[1]
    return pl.pallas_call(
        score_kernel,
        out_shape=[
            jax.ShapeDtypeStruct((tiles, channels + 2 * hidden), BF16),
            jax.ShapeDtypeStruct((tiles, hidden + LANES + 2 * channels), F32),
            jax.ShapeDtypeStruct((8, lanes), F32),
        ],
        compiler_params=pltpu.CompilerParams(vmem_limit_bytes=VMEM_LIMIT),
        name="tile_scores",
    )(pooled, slide, attn_v, attn_u, attn_w, class_t)


def merge(one, other):
    total = one[0:1] + other[0:1]
    safe = jnp.where(total > 0, total, 1.0)
    mean = one * (one[0:1] / safe) + other * (other[0:1] / safe)
    row = lax.broadcasted_iota(jnp.int32, one.shape, 0)
    return jnp.where(row == 0, total, mean)


def grads_kernel(
    packets,
    slides,
    shards,
    sides,
    positions,
    where,
    *refs,
):
    inputs, refs = refs[:sides], refs[sides:]
    boxes = refs[:packets]
    refs = refs[packets:]
    narrows, wides, refs = refs[:sides], refs[sides : 2 * sides], refs[2 * sides :]
    (owner, label, class_t, d_pre_out, term_keep, term_send, logit_out, loss_out, masks, sems) = refs
    blocks, block, channels = masks.shape
    per_side = blocks // sides
    fetches = [
        pltpu.make_async_copy(
            inputs[i // per_side].at[pl.ds(i % per_side * block, block)], masks.at[i], sems.at[i]
        )
        for i in range(blocks)
    ]
    for fetch in fetches:
        fetch.start()
    packet = boxes[0][...]
    for box in boxes[1:]:
        packet = merge(packet, box[...])
    classes = class_t.shape[0]
    lanes = packet.shape[1]
    total = packet[0:1]
    live = lax.broadcasted_iota(jnp.int32, (1, lanes), 1) < slides
    logits = [jnp.where(live, packet[k + 1 : k + 2], 0.0) for k in range(classes)]
    exp_logits = [jnp.exp(v) for v in logits]
    class_sum = functools.reduce(jnp.add, exp_logits)
    hot = [jnp.where(label[...] == k, 1.0, 0.0) for k in range(classes)]
    picked = functools.reduce(jnp.add, [v * h for v, h in zip(logits, hot)])
    loss = jnp.where(live, jnp.log(class_sum) - picked, 0.0)
    loss_out[...] = jnp.broadcast_to(jnp.sum(loss, axis=1, keepdims=True) / slides, loss_out.shape)
    d_logits = [jnp.where(live, (e / class_sum - h) / slides, 0.0) for e, h in zip(exp_logits, hot)]
    centre = functools.reduce(jnp.add, [d * v for d, v in zip(d_logits, logits)])

    mine = jnp.where((owner[...] == where[0]) & live, 1.0, 0.0)
    up = lax.broadcasted_iota(jnp.int32, (lanes, lanes), 0)
    across = lax.broadcasted_iota(jnp.int32, (lanes, lanes), 1)
    rank = jnp.dot(
        jnp.broadcast_to(mine, (8, lanes)), jnp.where(up < across, 1.0, 0.0), preferred_element_type=F32
    )
    wanted = lax.broadcasted_iota(jnp.int32, (8, lanes), 0).astype(F32)
    chosen = jnp.where((rank == wanted) & (mine > 0), 1.0, 0.0)
    column = lax.broadcasted_iota(jnp.int32, (8, LANES), 1)
    rows = jnp.zeros((8, LANES), F32)
    for k in range(classes):
        rows = jnp.where(column == k, jnp.sum(chosen * logits[k], axis=1, keepdims=True), rows)
    logit_out[...] = rows

    hidden = wides[0].shape[1] - LANES - 2 * channels

    def tile_terms(wide):
        stats = wide[:, hidden : hidden + LANES]
        member = member_of(stats[:, classes + 1 : classes + 2].astype(jnp.int32), lanes)

        def of_tile(row):
            return jnp.sum(member * row, axis=1, keepdims=True)

        weight = stats[:, 0:1] / of_tile(total)
        d_tile = [of_tile(d) for d in d_logits]
        d_weight = functools.reduce(jnp.add, [d * stats[:, k + 1 : k + 2] for k, d in enumerate(d_tile)])
        return weight.astype(BF16).astype(F32), d_tile, weight * (d_weight - of_tile(centre))

    terms = [tile_terms(wide) for wide in wides]
    count = block // positions
    for side in range(sides):
        kept, d_tile, d_score = terms[side]
        d_rows = functools.reduce(jnp.add, [d * class_t[k : k + 1, :] for k, d in enumerate(d_tile)])
        back = wides[side][:, hidden + LANES + channels :]
        d_emb = (kept * d_rows + d_score * back).astype(BF16).astype(F32)
        unit, inv = normal(wides[side][:, hidden + LANES : hidden + LANES + channels])
        d_pool = inv * (
            d_emb
            - jnp.mean(d_emb, axis=-1, keepdims=True)
            - unit * jnp.mean(d_emb * unit, axis=-1, keepdims=True)
        )
        scaled = (d_pool * (1.0 / positions)).astype(BF16)
        for j in range(per_side):
            i = side * per_side + j
            fetches[i].wait()
            here = masks[i].reshape(count, positions, channels)
            mine = scaled[j * count : (j + 1) * count]
            d_pre_out[i * block : (i + 1) * block] = (here * mine[:, None, :]).reshape(block, channels)

    smalls = [0.0] * classes
    wide_sum = 0.0
    embs, d_pres = [], []
    for (kept, d_tile, d_score), narrow, wide in zip(terms, narrows, wides):
        emb = narrow[:, :channels]
        emb32 = emb.astype(F32)
        for k in range(classes):
            smalls[k] = smalls[k] + jnp.sum(emb32 * (kept * d_tile[k]), axis=0, keepdims=True)
        wide_sum = wide_sum + jnp.sum(wide[:, :hidden] * d_score, axis=0, keepdims=True)
        embs.append(emb)
        d_pres.append((d_score * narrow[:, channels:].astype(F32)).astype(BF16))
    smalls.append(jnp.concatenate([wide_sum, jnp.zeros((1, hidden), F32)], axis=1))
    emb16 = jnp.concatenate(embs, axis=0)
    d_pre = jnp.concatenate(d_pres, axis=0)
    term = lax.dot_general(emb16, d_pre, (((0,), (0,)), ((), ())), preferred_element_type=F32)
    zs, ys, cs = shards
    share = channels // (zs * ys * cs)
    y, c = where[1], where[2]
    small = jnp.concatenate(smalls + [jnp.zeros((EXTRA - len(smalls), 2 * hidden), F32)], axis=0)
    if sides == 1:
        term_keep[:channels] = term
        term_keep[channels:] = small
        term_send[...] = jnp.zeros_like(term_send)
        return
    base = zs * share
    term_keep[base:] = small
    term_send[base:] = halves(small, len(smalls))
    for iy in range(ys):
        for ic in range(cs):
            starts = [((iz * ys + iy) * cs + ic) * share for iz in range(zs)]
            rows = jnp.concatenate([term[at : at + share] for at in starts], axis=0)

            @pl.when((c == ic) & (y == iy))
            def _():
                term_keep[:base] = rows

            @pl.when((c == ic) & (y != iy))
            def _():
                term_send[:base] = rows.astype(BF16)


def halves(small, count):
    high = small.astype(BF16).astype(F32)
    low = small - high
    return jnp.concatenate([high[:count], low[:count], jnp.zeros_like(small[2 * count :])], axis=0).astype(BF16)


def joined(rows, count):
    wide = rows.astype(F32)
    return jnp.concatenate([wide[:count] + wide[count : 2 * count], jnp.zeros_like(wide[count:])], axis=0)


def deep_kernel(count, steps, where, keep, got, own, *away):
    share = own.shape[0] - EXTRA
    zs = len(steps) + 1
    small = keep[zs * share :] + joined(got[zs * share :], count)
    split = halves(small, count)
    for step, out in zip((0, *steps), (own, *away)):
        at = pl.ds(pl.multiple_of((where[0] + step) % zs * share, share), share)
        block = keep[at, :] + got[at, :].astype(F32)
        out[:share] = block.astype(out.dtype)
        out[share:] = small if step == 0 else split


def deep_fold(where, keep, got, steps, count):
    zs = len(steps) + 1
    shape = ((keep.shape[0] - EXTRA) // zs + EXTRA, keep.shape[1])
    return pl.pallas_call(
        functools.partial(deep_kernel, count, steps),
        in_specs=[pl.BlockSpec(memory_space=pltpu.SMEM)] + [pl.BlockSpec(memory_space=pltpu.VMEM)] * 2,
        out_shape=[jax.ShapeDtypeStruct(shape, F32)] + [jax.ShapeDtypeStruct(shape, BF16)] * len(steps),
        compiler_params=pltpu.CompilerParams(vmem_limit_bytes=VMEM_LIMIT),
        name="attention_deep",
    )(where, keep, got)


def last_kernel(count, own, *rest):
    got, (v_out, u_out, small_out) = rest[:-3], rest[-3:]
    share, hidden = v_out.shape
    block = own[:share]
    small = own[share:]
    for one in got:
        block = block + one[:share].astype(F32)
        small = small + joined(one[share:], count)
    v_out[...] = block[:, :hidden]
    u_out[...] = block[:, hidden:]
    small_out[...] = small


def last_fold(own, got, count):
    share, hidden = own.shape[0] - EXTRA, own.shape[1] // 2
    return pl.pallas_call(
        functools.partial(last_kernel, count),
        out_shape=[
            jax.ShapeDtypeStruct((share, hidden), F32),
            jax.ShapeDtypeStruct((share, hidden), F32),
            jax.ShapeDtypeStruct((EXTRA, own.shape[1]), F32),
        ],
        compiler_params=pltpu.CompilerParams(vmem_limit_bytes=VMEM_LIMIT),
        name="attention_last",
    )(own, *got)


def grads(where, masks, boxes, narrows, wides, owner, label, class_t, slides, shards, positions):
    rows, channels = masks[0].shape
    hidden = wides[0].shape[1] - LANES - 2 * channels
    zs, ys, cs = shards
    sides = len(narrows)
    keep_shape = (channels // (ys * cs) + EXTRA, 2 * hidden)
    send_shape = keep_shape if sides > 1 else (16, LANES)
    block = 8 * positions if rows % (8 * positions) == 0 else rows
    operands = [where, *map(in_hbm, masks), *boxes, *narrows, *wides, owner, label, class_t]
    return pl.pallas_call(
        functools.partial(grads_kernel, len(boxes), slides, shards, sides, positions),
        in_specs=[IN_SMEM] + [IN_HBM] * sides + [IN_VMEM] * (len(operands) - 1 - sides),
        out_shape=[
            jax.ShapeDtypeStruct((sides * rows, channels), BF16),
            jax.ShapeDtypeStruct(keep_shape, F32),
            jax.ShapeDtypeStruct(send_shape, BF16),
            jax.ShapeDtypeStruct((8, LANES), F32),
            jax.ShapeDtypeStruct((8, LANES), F32),
        ],
        scratch_shapes=[
            pltpu.VMEM((sides * rows // block, block, channels), BF16),
            pltpu.SemaphoreType.DMA((sides * rows // block,)),
        ],
        compiler_params=pltpu.CompilerParams(vmem_limit_bytes=VMEM_LIMIT),
        name="head_grads",
    )(*operands)


def backward_kernel(ys, parts, where, token, d_pre, *refs):
    tiles, refs = refs[:parts], refs[parts:]
    near, over, refs = refs[0], refs[1], refs[2:]
    _, columns, sems = refs
    sides, rows, width = columns.shape
    share = width // ys
    y = where[1]
    across = pl.ds(pl.multiple_of(where[0] * width, width), width)
    fetches = [pltpu.make_async_copy(tiles[i].at[:, across], columns.at[i], sems.at[i]) for i in range(sides)]
    for fetch in fetches:
        fetch.start()
    contract = (((0,), (0,)), ((), ()))
    term = 0.0
    for i in range(0, sides, 2):
        fetches[i].wait()
        fetches[i + 1].wait()
        both = columns[i : i + 2].reshape(2 * rows, width)
        term = term + lax.dot_general(
            both, d_pre[i * rows : (i + 2) * rows], contract, preferred_element_type=F32
        )
    for iy in range(ys):
        block = term[iy * share : (iy + 1) * share]

        @pl.when(y == iy)
        def _():
            near[...] = block

        @pl.when(y != iy)
        def _():
            over[...] = block.astype(BF16)


def backward_chunk(where, token, tiles, d_pre, ys, share):
    rows = tiles[0].shape[0]
    channels = d_pre.shape[1]
    width = ys * share
    operands = [where, token, d_pre, *map(in_hbm, tiles)]
    return pl.pallas_call(
        functools.partial(backward_kernel, ys, len(tiles)),
        in_specs=[IN_SMEM, ANYWHERE, IN_VMEM] + [IN_HBM] * len(tiles),
        out_specs=[IN_VMEM, IN_VMEM, ANYWHERE],
        scratch_shapes=[
            pltpu.VMEM((len(tiles), rows, width), BF16),
            pltpu.SemaphoreType.DMA((len(tiles),)),
        ],
        out_shape=[
            jax.ShapeDtypeStruct((share, channels), F32),
            jax.ShapeDtypeStruct((share, channels), BF16),
            jax.ShapeDtypeStruct(token.shape, token.dtype),
        ],
        input_output_aliases={1: 2},
        compiler_params=pltpu.CompilerParams(vmem_limit_bytes=VMEM_LIMIT),
        cost_estimate=pl.CostEstimate(
            flops=2 * len(tiles) * rows * width * channels,
            bytes_accessed=2 * len(tiles) * rows * width,
            transcendentals=0,
        ),
        name="section_backward",
    )(*operands)


def sum_fold(near, got, dtype):
    total = near
    for one in got:
        total = total + one.astype(F32)
    return total.astype(dtype)


def grid_of(devices):
    return (4, 2, 2) if devices == 16 else None


def moves(shape):
    zs, ys, cs = shape

    def at(z, y, c):
        return (z * ys + y) * cs + c

    every = [(z, y, c) for z in range(zs) for y in range(ys) for c in range(cs)]
    def pair(bits):
        return [(at(*i), at(i[0] ^ bits, i[1], i[2])) for i in every]

    core = [(at(*i), at(i[0], i[1], i[2] ^ 1)) for i in every]
    row = [(at(*i), at(i[0], i[1] ^ 1, i[2])) for i in every]

    def deep(step):
        return [(at(*i), at((i[0] + step) % zs, i[1], i[2])) for i in every]

    return core, row, deep, pair


def together(*values):
    return lax.optimization_barrier(values)


def send(x, pairs):
    return lax.ppermute(x, "dp", pairs)


def per_device(tiles, conv_weight, tile_slide, slide_owner, labels, attn_v, attn_u, attn_w, class_w):
    tile_count, positions, inputs = tiles.shape
    share, channels = conv_weight.shape
    hidden = attn_v.shape[1]
    classes = class_w.shape[1]
    slides = slide_owner.shape[0]
    devices = lax.axis_size("dp")
    me = lax.axis_index("dp")
    shape = grid_of(devices)
    rows = tile_count * positions
    plain_rows = tiles.reshape(rows, inputs)
    tile_rows = in_hbm(plain_rows)
    lanes = -(-slides // LANES) * LANES
    pad = lanes - slides
    slide = tile_slide[:, None]
    owner = jnp.pad(slide_owner, (0, pad), constant_values=-1)[None, :]
    label = jnp.pad(labels, (0, pad), constant_values=-1)[None, :]
    class_t = class_w.T
    attn_w_row = attn_w[None, :]

    token = jnp.zeros((8, LANES), F32)
    if shape is None:
        where = jnp.zeros((2,), jnp.int32)
        gathered = lax.all_gather(conv_weight, "dp", axis=0, tiled=True)
        mask, pooled, token = forward_chunk(where, token, tile_rows, [gathered], None, True, positions)
    else:
        zs, ys, cs = shape
        core, row, deep, pair = moves(shape)
        z, y, c = me // (ys * cs), me // cs % ys, me % cs
        own_parts, away_parts = [], []

        def block(step, near, pieces):
            spot = (z - step) % zs * ys + (y if near else y ^ 1)
            return spot, pieces

        mine, across, mine_core = conv_weight, send(conv_weight, row), send(conv_weight, core)
        acc, waiting, last = None, [], zs - 1
        for step in range(zs):
            if step < last:
                ahead = send(mine, deep(1))
                extra = []
                if step < 2:
                    extra += split_inputs(c, tile_rows, cs, share, step, 2)
                if step > 0:
                    extra.append(away_parts[step - 1])
                    extra.append(across_core)
                across, ahead, mine_core, token, *extra = together(across, ahead, mine_core, token, *extra)
                if step > 0:
                    landed = extra.pop()
                    if waiting:
                        waiting[-1][1][1] = landed
                    away_parts[step - 1] = in_hbm(extra.pop())
                ahead_across, ahead_core = send(ahead, row), send(ahead, core)
                across_core = send(across, core)
                waiting.append(block(step, True, [mine, mine_core]))
                waiting.append(block(step, False, [across, across_core]))
                if step < 2:
                    own_parts.append(extra[0])
                    if step == 1:
                        across_core, extra[1] = together(across_core, extra[1])
                        waiting[-1] = block(step, False, [across, across_core])
                    away_parts.append(send(extra[1], core))
                if step == last - 1:
                    waiting.append(block(last, True, [ahead, ahead_core]))
                mine, across, mine_core = ahead, ahead_across, ahead_core
            else:
                across, token = together(across, token)
                waiting.append(block(last, False, [across, send(across, core)]))
            if step > 0:
                groups = [spot for spot, _ in waiting]
                order = [i * cs + (c ^ k) for i in range(len(groups)) for k in range(cs)]
                where = jnp.stack([*groups, *order]).astype(jnp.int32)
                pieces = [piece for _, pair in waiting for piece in pair]
                *out, token = forward_chunk(
                    where, token, tile_rows, pieces, acc, step == last, positions, len(groups)
                )
                acc, waiting = out[0], []
        mask, pooled = out

    narrow, wide, packet = score(pooled, slide, attn_v, attn_u, attn_w_row, class_t, lanes)
    narrows, wides, masks = [narrow], [wide], [mask]
    if shape is None:
        boxes = lax.all_gather(packet, "dp", axis=0)
        boxes = [boxes[i] for i in range(devices)]
        where = jnp.stack([me, me, me]).astype(jnp.int32)
    else:
        packet = merge(packet, send(packet, core))
        packet = merge(packet, send(packet, row))
        packet, *ours = together(packet, narrow, wide, mask)
        for group, one in zip((narrows, wides, masks), ours):
            group[0] = one
            group.append(send(one, core))
        boxes = [packet] + [send(packet, deep(i)) for i in (2, 1, 3)]
        where = jnp.stack([me, y, c]).astype(jnp.int32)
    d_pre, term_keep, term_send, logit_rows, loss_rows = grads(
        where, masks, boxes, narrows, wides, owner, label, class_t, slides, shape or (1, 1, 1), positions
    )
    slides_here = slides // devices
    logits = logit_rows[:slides_here, :classes]
    loss = loss_rows[0, :1]

    if shape is None:
        contract = (((0,), (0,)), ((), ()))
        term = lax.dot_general(plain_rows, d_pre, contract, preferred_element_type=F32)
        conv_grad = lax.psum_scatter(term, "dp", scatter_dimension=0, tiled=True)
        pair = lax.psum_scatter(term_keep[:channels], "dp", scatter_dimension=0, tiled=True)
        small = jnp.sum(lax.all_gather(term_keep[channels:], "dp", axis=0), axis=0)
        return (conv_grad, pair[:, :hidden], pair[:, hidden:], small[classes, :hidden], small[:classes].T, logits, loss)

    extra = classes + 1
    steps = (2, 1, 3)
    term_send, token = together(term_send, token)
    attn_got = send(term_send, row)

    where = [jnp.stack([z ^ bits, y, c]).astype(jnp.int32) for bits in range(zs)]

    parts = own_parts + away_parts

    def chunk(bits, d_pre, token):
        near, over, token = backward_chunk(where[bits], token, parts, d_pre, ys, share)
        return near, over, d_pre, token

    near_both, over_both, d_pre, token = chunk(3, d_pre, token)
    over_both, attn_got, token = together(over_both, attn_got, token)
    y_both = send(over_both, row)
    near_far, over_far, d_pre, token = chunk(2, d_pre, token)
    over_far, attn_got, token = together(over_far, attn_got, token)
    y_far = send(over_far, row)
    own, *away = deep_fold(z[None], term_keep, attn_got, steps, extra)
    attn = [send(block, deep(i)) for i, block in zip(steps, away)]
    out_both, token, *_ = together(sum_fold(near_both, [y_both], BF16), token)
    z_both = send(out_both, pair(1))
    near_next, over_next, d_pre, token = chunk(1, d_pre, token)
    over_next, y_far, token, *attn = together(over_next, y_far, token, *attn)
    y_next = send(over_next, row)
    half = share // 2
    outs = [sum_fold(near_far[at], [y_far[at], z_both[at]], BF16) for at in (slice(half), slice(half, None))]
    *outs, token = together(*outs, token)
    z_far = [send(out, pair(2)) for out in outs]
    near_own, over_own, d_pre, token = chunk(0, d_pre, token)
    over_own, y_next, z_far[0], token = together(over_own, y_next, z_far[0], token)
    y_own = send(over_own, row)
    z_next = send(sum_fold(near_next, [y_next], BF16), pair(1))
    own, near_own = together(own, near_own)
    v_grad, u_grad, small = last_fold(own, attn, extra)
    conv_grad = sum_fold(near_own, [y_own, z_next, jnp.concatenate(z_far, axis=0)], F32)
    return (conv_grad, v_grad, u_grad, small[classes, :hidden], small[:classes].T, logits, loss)


def solution(mesh):
    in_specs = (
        P(("groups", "dp"), None, None),
        P("dp", None),
        P(("groups", "dp")),
        P("groups"),
        P("groups"),
        P(),
        P(),
        P(),
        P(),
    )
    out_specs = (
        P(("groups", "dp"), None),
        P(("groups", "dp"), None),
        P(("groups", "dp"), None),
        P("groups"),
        P("groups", None),
        P(("groups", "dp"), None),
        P("groups"),
    )
    return jax.shard_map(per_device, mesh=mesh, in_specs=in_specs, out_specs=out_specs, check_vma=False)
```

```python
import functools

import jax
import jax.numpy as jnp
from jax import lax
from jax.experimental import pallas as pl
from jax.experimental.pallas import tpu as pltpu
from jax.sharding import PartitionSpec as P

norm_eps = 1e-05
F32 = jnp.float32
BF16 = jnp.bfloat16
LANES = 128
EXTRA = 16
VMEM_LIMIT = 32 * 1024 * 1024


IN_VMEM = pl.BlockSpec(memory_space=pltpu.VMEM)
IN_SMEM = pl.BlockSpec(memory_space=pltpu.SMEM)
IN_HBM = pl.BlockSpec(memory_space=pltpu.HBM)
ANYWHERE = pl.BlockSpec(memory_space=pl.ANY)


def in_hbm(x):
    return pltpu.with_memory_space_constraint(x, pltpu.HBM)


def split_kernel(cs, share, where, tiles, own, away):
    inputs = tiles.shape[1]
    c = where[0]
    for ic in range(cs):
        starts = range(ic * share, inputs, cs * share)
        part = jnp.concatenate([tiles[:, at : at + share] for at in starts], axis=1)

        @pl.when(c == ic)
        def _():
            own[...] = part

        @pl.when(c != ic)
        def _():
            away[...] = part


def split_inputs(c, tile_rows, cs, share, part, parts):
    rows, inputs = tile_rows.shape
    rows = rows // parts
    block = min(rows, 256)
    skip = part * (rows // block)
    half = pl.BlockSpec((block, inputs // cs), lambda i: (i, 0))
    return pl.pallas_call(
        functools.partial(split_kernel, cs, share),
        grid=(rows // block,),
        in_specs=[IN_SMEM, pl.BlockSpec((block, inputs), lambda i: (skip + i, 0))],
        out_specs=[half, half],
        out_shape=[pltpu.HBM((rows, inputs // cs), BF16)] * 2,
        compiler_params=pltpu.CompilerParams(vmem_limit_bytes=VMEM_LIMIT),
        name="split_inputs",
    )(c[None].astype(jnp.int32), tile_rows)


def forward_kernel(groups, pieces, first, last, positions, where, token, tiles, *refs):
    ws = refs[:pieces]
    rest = refs[pieces:]
    if not first:
        acc_in, rest = rest[0], rest[1:]
    if last:
        mask_out, pooled_out, _, weight, rows_in, totals, sems, loads, masks = rest
    else:
        acc_out, _, weight, rows_in, totals, sems, loads = rest
    blocks, block, depth = rows_in.shape
    share = ws[0].shape[0]
    wide = depth // groups

    def here(i):
        return pl.ds(pl.multiple_of(i * block, block), block)

    def fetch(i, g):
        across = pl.ds(pl.multiple_of(where[g] * wide, wide), wide)
        to = rows_in.at[i, :, pl.ds(g * wide, wide)]
        return pltpu.make_async_copy(tiles.at[here(i), across], to, sems.at[3 + g, i])

    def load(i):
        start = pl.multiple_of(where[groups + i] * share, share)
        return pltpu.make_async_copy(ws[i], weight.at[pl.ds(start, share)], loads.at[i])

    def resume(i):
        return pltpu.make_async_copy(acc_in.at[here(i)], totals.at[i], sems.at[1, i])

    def store(i):
        if last:
            return pltpu.make_async_copy(masks.at[i], mask_out.at[here(i)], sems.at[2, i])
        return pltpu.make_async_copy(totals.at[i], acc_out.at[here(i)], sems.at[2, i])

    for i in range(blocks):
        for g in range(groups):
            fetch(i, g).start()
        if not first:
            resume(i).start()
    for i in range(pieces):
        load(i).start()
    for i in range(pieces):
        load(i).wait()
    count = block // positions

    @pl.loop(0, blocks)
    def _(i):
        for g in range(groups):
            fetch(i, g).wait()
        total = jnp.dot(rows_in[i], weight[...], preferred_element_type=F32)
        if not first:
            resume(i).wait()
            total = total + totals[i]
        if last:
            masks[i] = jnp.where(total > 0, 1.0, jnp.where(total == 0, 0.5, 0.0)).astype(BF16)
            active = jnp.maximum(total, 0.0).reshape(count, positions, total.shape[1])
            pooled_out[pl.ds(pl.multiple_of(i * count, count), count), :] = jnp.sum(active, axis=1) * (1.0 / positions)
        else:
            totals[i] = total
        store(i).start()

    for i in range(blocks):
        store(i).wait()


def forward_chunk(where, token, tile_rows, ws, acc, last, positions, groups=1):
    rows, inputs = tile_rows.shape
    share, channels = ws[0].shape
    pieces = len(ws)
    depth = share * pieces
    block = 8 * positions if rows % (8 * positions) == 0 else rows
    first = acc is None
    in_specs = [IN_SMEM, ANYWHERE, IN_HBM] + [ANYWHERE] * pieces
    operands = [where, token, tile_rows, *ws]
    alias = {}
    if not first:
        in_specs.append(IN_HBM)
        operands.append(in_hbm(acc))
    if last:
        out_shape = [
            pltpu.HBM((rows, channels), BF16),
            jax.ShapeDtypeStruct((rows // positions, channels), F32),
        ]
        out_specs = [IN_HBM, IN_VMEM]
    else:
        out_shape = [pltpu.HBM((rows, channels), F32)]
        out_specs = [IN_HBM]
        if not first:
            alias = {len(operands) - 1: 0}
    alias[1] = len(out_shape)
    out_specs.append(ANYWHERE)
    out_shape.append(jax.ShapeDtypeStruct(token.shape, token.dtype))
    blocks = rows // block
    scratch = [
        pltpu.VMEM((depth, channels), BF16),
        pltpu.VMEM((blocks, block, depth), BF16),
        pltpu.VMEM((blocks, block, channels) if not (first and last) else (1, 8, LANES), F32),
        pltpu.SemaphoreType.DMA((3 + groups, blocks)),
        pltpu.SemaphoreType.DMA((pieces,)),
    ]
    if last:
        scratch.append(pltpu.VMEM((blocks, block, channels), BF16))
    return pl.pallas_call(
        functools.partial(forward_kernel, groups, pieces, first, last, positions),
        in_specs=in_specs,
        out_specs=out_specs,
        scratch_shapes=scratch,
        out_shape=out_shape,
        input_output_aliases=alias,
        compiler_params=pltpu.CompilerParams(vmem_limit_bytes=VMEM_LIMIT if depth < inputs else 2 * VMEM_LIMIT - 2**22),
        cost_estimate=pl.CostEstimate(
            flops=2 * rows * depth * channels,
            bytes_accessed=2 * rows * depth,
            transcendentals=0,
        ),
        name="section_forward",
    )(*operands)


def member_of(tile_slide, lanes):
    slide = lax.broadcasted_iota(jnp.int32, (tile_slide.shape[0], lanes), 1)
    return (tile_slide == slide).astype(F32)


def normal(pooled):
    centred = pooled - jnp.mean(pooled, axis=-1, keepdims=True)
    spread = jnp.mean(centred * centred, axis=-1, keepdims=True)
    scale = lax.rsqrt(spread + norm_eps)
    return centred * scale, scale


def score_kernel(pooled, slide, attn_v, attn_u, attn_w, class_t, narrow_out, wide_out, packet_out):
    channels, hidden = attn_v.shape
    unit, _ = normal(pooled[...])
    emb = unit.astype(BF16)
    narrow_out[:, :channels] = emb
    act_a = jnp.tanh(jnp.dot(emb, attn_v[...], preferred_element_type=F32))
    act_g = jax.nn.sigmoid(jnp.dot(emb, attn_u[...], preferred_element_type=F32))
    gated = act_a * act_g
    wide_out[:, :hidden] = gated
    exp_score = jnp.exp(jnp.sum(gated * attn_w[...], axis=1, keepdims=True))
    emb32 = emb.astype(F32)
    classes = class_t.shape[0]
    reads = [jnp.sum(emb32 * class_t[k : k + 1, :], axis=1, keepdims=True) for k in range(classes)]
    lanes = packet_out.shape[1]
    member = member_of(slide[...], lanes)
    total = jnp.sum(member * exp_score, axis=0, keepdims=True)
    own_total = jnp.sum(member * total, axis=1, keepdims=True)
    part = jnp.where(own_total > 0, exp_score / own_total, 0.0)
    packet_out[...] = jnp.zeros_like(packet_out)
    packet_out[0:1, :] = total
    for k in range(classes):
        packet_out[k + 1 : k + 2, :] = jnp.sum(member * (part * reads[k]), axis=0, keepdims=True)
    column = lax.broadcasted_iota(jnp.int32, (emb.shape[0], LANES), 1)
    stats = jnp.where(column == 0, exp_score, 0.0)
    for k in range(classes):
        stats = jnp.where(column == k + 1, reads[k], stats)
    wide_out[:, hidden : hidden + LANES] = jnp.where(column == classes + 1, slide[...].astype(F32), stats)
    ua = (attn_w[...] * act_g * (1.0 - act_a * act_a)).astype(BF16)
    ug = (attn_w[...] * act_a * act_g * (1.0 - act_g)).astype(BF16)
    narrow_out[:, channels : channels + hidden] = ua
    narrow_out[:, channels + hidden :] = ug
    contract = (((1,), (1,)), ((), ()))
    wide_out[:, hidden + LANES : hidden + LANES + channels] = pooled[...]
    wide_out[:, hidden + LANES + channels :] = lax.dot_general(ua, attn_v[...], contract, preferred_element_type=F32) + lax.dot_general(
        ug, attn_u[...], contract, preferred_element_type=F32
    )


def score(pooled, slide, attn_v, attn_u, attn_w, class_t, lanes):
    tiles, channels = pooled.shape
    hidden = attn_v.shape[1]
    return pl.pallas_call(
        score_kernel,
        out_shape=[
            jax.ShapeDtypeStruct((tiles, channels + 2 * hidden), BF16),
            jax.ShapeDtypeStruct((tiles, hidden + LANES + 2 * channels), F32),
            jax.ShapeDtypeStruct((8, lanes), F32),
        ],
        compiler_params=pltpu.CompilerParams(vmem_limit_bytes=VMEM_LIMIT),
        name="tile_scores",
    )(pooled, slide, attn_v, attn_u, attn_w, class_t)


def merge(one, other):
    total = one[0:1] + other[0:1]
    safe = jnp.where(total > 0, total, 1.0)
    mean = one * (one[0:1] / safe) + other * (other[0:1] / safe)
    row = lax.broadcasted_iota(jnp.int32, one.shape, 0)
    return jnp.where(row == 0, total, mean)


def grads_kernel(
    packets,
    slides,
    shards,
    sides,
    positions,
    where,
    *refs,
):
    inputs, refs = refs[:sides], refs[sides:]
    boxes = refs[:packets]
    refs = refs[packets:]
    narrows, wides, refs = refs[:sides], refs[sides : 2 * sides], refs[2 * sides :]
    (owner, label, class_t, d_pre_out, term_keep, term_send, logit_out, loss_out, masks, sems) = refs
    blocks, block, channels = masks.shape
    per_side = blocks // sides
    fetches = [
        pltpu.make_async_copy(
            inputs[i // per_side].at[pl.ds(i % per_side * block, block)], masks.at[i], sems.at[i]
        )
        for i in range(blocks)
    ]
    for fetch in fetches:
        fetch.start()
    packet = boxes[0][...]
    for box in boxes[1:]:
        packet = merge(packet, box[...])
    classes = class_t.shape[0]
    lanes = packet.shape[1]
    total = packet[0:1]
    live = lax.broadcasted_iota(jnp.int32, (1, lanes), 1) < slides
    logits = [jnp.where(live, packet[k + 1 : k + 2], 0.0) for k in range(classes)]
    exp_logits = [jnp.exp(v) for v in logits]
    class_sum = functools.reduce(jnp.add, exp_logits)
    hot = [jnp.where(label[...] == k, 1.0, 0.0) for k in range(classes)]
    picked = functools.reduce(jnp.add, [v * h for v, h in zip(logits, hot)])
    loss = jnp.where(live, jnp.log(class_sum) - picked, 0.0)
    loss_out[...] = jnp.broadcast_to(jnp.sum(loss, axis=1, keepdims=True) / slides, loss_out.shape)
    d_logits = [jnp.where(live, (e / class_sum - h) / slides, 0.0) for e, h in zip(exp_logits, hot)]
    centre = functools.reduce(jnp.add, [d * v for d, v in zip(d_logits, logits)])

    mine = jnp.where((owner[...] == where[0]) & live, 1.0, 0.0)
    up = lax.broadcasted_iota(jnp.int32, (lanes, lanes), 0)
    across = lax.broadcasted_iota(jnp.int32, (lanes, lanes), 1)
    rank = jnp.dot(
        jnp.broadcast_to(mine, (8, lanes)), jnp.where(up < across, 1.0, 0.0), preferred_element_type=F32
    )
    wanted = lax.broadcasted_iota(jnp.int32, (8, lanes), 0).astype(F32)
    chosen = jnp.where((rank == wanted) & (mine > 0), 1.0, 0.0)
    column = lax.broadcasted_iota(jnp.int32, (8, LANES), 1)
    rows = jnp.zeros((8, LANES), F32)
    for k in range(classes):
        rows = jnp.where(column == k, jnp.sum(chosen * logits[k], axis=1, keepdims=True), rows)
    logit_out[...] = rows

    hidden = wides[0].shape[1] - LANES - 2 * channels

    def tile_terms(wide):
        stats = wide[:, hidden : hidden + LANES]
        member = member_of(stats[:, classes + 1 : classes + 2].astype(jnp.int32), lanes)

        def of_tile(row):
            return jnp.sum(member * row, axis=1, keepdims=True)

        weight = stats[:, 0:1] / of_tile(total)
        d_tile = [of_tile(d) for d in d_logits]
        d_weight = functools.reduce(jnp.add, [d * stats[:, k + 1 : k + 2] for k, d in enumerate(d_tile)])
        return weight.astype(BF16).astype(F32), d_tile, weight * (d_weight - of_tile(centre))

    terms = [tile_terms(wide) for wide in wides]
    count = block // positions
    for side in range(sides):
        kept, d_tile, d_score = terms[side]
        d_rows = functools.reduce(jnp.add, [d * class_t[k : k + 1, :] for k, d in enumerate(d_tile)])
        back = wides[side][:, hidden + LANES + channels :]
        d_emb = (kept * d_rows + d_score * back).astype(BF16).astype(F32)
        unit, inv = normal(wides[side][:, hidden + LANES : hidden + LANES + channels])
        d_pool = inv * (
            d_emb
            - jnp.mean(d_emb, axis=-1, keepdims=True)
            - unit * jnp.mean(d_emb * unit, axis=-1, keepdims=True)
        )
        scaled = (d_pool * (1.0 / positions)).astype(BF16)
        for j in range(per_side):
            i = side * per_side + j
            fetches[i].wait()
            here = masks[i].reshape(count, positions, channels)
            mine = scaled[j * count : (j + 1) * count]
            d_pre_out[i * block : (i + 1) * block] = (here * mine[:, None, :]).reshape(block, channels)

    smalls = [0.0] * classes
    wide_sum = 0.0
    embs, d_pres = [], []
    for (kept, d_tile, d_score), narrow, wide in zip(terms, narrows, wides):
        emb = narrow[:, :channels]
        emb32 = emb.astype(F32)
        for k in range(classes):
            smalls[k] = smalls[k] + jnp.sum(emb32 * (kept * d_tile[k]), axis=0, keepdims=True)
        wide_sum = wide_sum + jnp.sum(wide[:, :hidden] * d_score, axis=0, keepdims=True)
        embs.append(emb)
        d_pres.append((d_score * narrow[:, channels:].astype(F32)).astype(BF16))
    smalls.append(jnp.concatenate([wide_sum, jnp.zeros((1, hidden), F32)], axis=1))
    emb16 = jnp.concatenate(embs, axis=0)
    d_pre = jnp.concatenate(d_pres, axis=0)
    term = lax.dot_general(emb16, d_pre, (((0,), (0,)), ((), ())), preferred_element_type=F32)
    zs, ys, cs = shards
    share = channels // (zs * ys * cs)
    y, c = where[1], where[2]
    small = jnp.concatenate(smalls + [jnp.zeros((EXTRA - len(smalls), 2 * hidden), F32)], axis=0)
    if sides == 1:
        term_keep[:channels] = term
        term_keep[channels:] = small
        term_send[...] = jnp.zeros_like(term_send)
        return
    base = zs * share
    term_keep[base:] = small
    term_send[base:] = halves(small, len(smalls))
    for iy in range(ys):
        for ic in range(cs):
            starts = [((iz * ys + iy) * cs + ic) * share for iz in range(zs)]
            rows = jnp.concatenate([term[at : at + share] for at in starts], axis=0)

            @pl.when((c == ic) & (y == iy))
            def _():
                term_keep[:base] = rows

            @pl.when((c == ic) & (y != iy))
            def _():
                term_send[:base] = rows.astype(BF16)


def halves(small, count):
    high = small.astype(BF16).astype(F32)
    low = small - high
    return jnp.concatenate([high[:count], low[:count], jnp.zeros_like(small[2 * count :])], axis=0).astype(BF16)


def joined(rows, count):
    wide = rows.astype(F32)
    return jnp.concatenate([wide[:count] + wide[count : 2 * count], jnp.zeros_like(wide[count:])], axis=0)


def deep_kernel(count, steps, where, keep, got, own, *away):
    share = own.shape[0] - EXTRA
    zs = len(steps) + 1
    small = keep[zs * share :] + joined(got[zs * share :], count)
    split = halves(small, count)
    for step, out in zip((0, *steps), (own, *away)):
        at = pl.ds(pl.multiple_of((where[0] + step) % zs * share, share), share)
        block = keep[at, :] + got[at, :].astype(F32)
        out[:share] = block.astype(out.dtype)
        out[share:] = small if step == 0 else split


def deep_fold(where, keep, got, steps, count):
    zs = len(steps) + 1
    shape = ((keep.shape[0] - EXTRA) // zs + EXTRA, keep.shape[1])
    return pl.pallas_call(
        functools.partial(deep_kernel, count, steps),
        in_specs=[pl.BlockSpec(memory_space=pltpu.SMEM)] + [pl.BlockSpec(memory_space=pltpu.VMEM)] * 2,
        out_shape=[jax.ShapeDtypeStruct(shape, F32)] + [jax.ShapeDtypeStruct(shape, BF16)] * len(steps),
        compiler_params=pltpu.CompilerParams(vmem_limit_bytes=VMEM_LIMIT),
        name="attention_deep",
    )(where, keep, got)


def last_kernel(count, own, *rest):
    got, (v_out, u_out, small_out) = rest[:-3], rest[-3:]
    share, hidden = v_out.shape
    block = own[:share]
    small = own[share:]
    for one in got:
        block = block + one[:share].astype(F32)
        small = small + joined(one[share:], count)
    v_out[...] = block[:, :hidden]
    u_out[...] = block[:, hidden:]
    small_out[...] = small


def last_fold(own, got, count):
    share, hidden = own.shape[0] - EXTRA, own.shape[1] // 2
    return pl.pallas_call(
        functools.partial(last_kernel, count),
        out_shape=[
            jax.ShapeDtypeStruct((share, hidden), F32),
            jax.ShapeDtypeStruct((share, hidden), F32),
            jax.ShapeDtypeStruct((EXTRA, own.shape[1]), F32),
        ],
        compiler_params=pltpu.CompilerParams(vmem_limit_bytes=VMEM_LIMIT),
        name="attention_last",
    )(own, *got)


def grads(where, masks, boxes, narrows, wides, owner, label, class_t, slides, shards, positions):
    rows, channels = masks[0].shape
    hidden = wides[0].shape[1] - LANES - 2 * channels
    zs, ys, cs = shards
    sides = len(narrows)
    keep_shape = (channels // (ys * cs) + EXTRA, 2 * hidden)
    send_shape = keep_shape if sides > 1 else (16, LANES)
    block = 8 * positions if rows % (8 * positions) == 0 else rows
    operands = [where, *map(in_hbm, masks), *boxes, *narrows, *wides, owner, label, class_t]
    return pl.pallas_call(
        functools.partial(grads_kernel, len(boxes), slides, shards, sides, positions),
        in_specs=[IN_SMEM] + [IN_HBM] * sides + [IN_VMEM] * (len(operands) - 1 - sides),
        out_shape=[
            jax.ShapeDtypeStruct((sides * rows, channels), BF16),
            jax.ShapeDtypeStruct(keep_shape, F32),
            jax.ShapeDtypeStruct(send_shape, BF16),
            jax.ShapeDtypeStruct((8, LANES), F32),
            jax.ShapeDtypeStruct((8, LANES), F32),
        ],
        scratch_shapes=[
            pltpu.VMEM((sides * rows // block, block, channels), BF16),
            pltpu.SemaphoreType.DMA((sides * rows // block,)),
        ],
        compiler_params=pltpu.CompilerParams(vmem_limit_bytes=VMEM_LIMIT),
        name="head_grads",
    )(*operands)


def backward_kernel(ys, parts, where, token, d_pre, *refs):
    tiles, refs = refs[:parts], refs[parts:]
    near, over, refs = refs[0], refs[1], refs[2:]
    _, columns, sems = refs
    sides, rows, width = columns.shape
    share = width // ys
    y = where[1]
    across = pl.ds(pl.multiple_of(where[0] * width, width), width)
    fetches = [pltpu.make_async_copy(tiles[i].at[:, across], columns.at[i], sems.at[i]) for i in range(sides)]
    for fetch in fetches:
        fetch.start()
    contract = (((0,), (0,)), ((), ()))
    term = 0.0
    for i in range(0, sides, 2):
        fetches[i].wait()
        fetches[i + 1].wait()
        both = columns[i : i + 2].reshape(2 * rows, width)
        term = term + lax.dot_general(
            both, d_pre[i * rows : (i + 2) * rows], contract, preferred_element_type=F32
        )
    for iy in range(ys):
        block = term[iy * share : (iy + 1) * share]

        @pl.when(y == iy)
        def _():
            near[...] = block

        @pl.when(y != iy)
        def _():
            over[...] = block.astype(BF16)


def backward_chunk(where, token, tiles, d_pre, ys, share):
    rows = tiles[0].shape[0]
    channels = d_pre.shape[1]
    width = ys * share
    operands = [where, token, d_pre, *map(in_hbm, tiles)]
    return pl.pallas_call(
        functools.partial(backward_kernel, ys, len(tiles)),
        in_specs=[IN_SMEM, ANYWHERE, IN_VMEM] + [IN_HBM] * len(tiles),
        out_specs=[IN_VMEM, IN_VMEM, ANYWHERE],
        scratch_shapes=[
            pltpu.VMEM((len(tiles), rows, width), BF16),
            pltpu.SemaphoreType.DMA((len(tiles),)),
        ],
        out_shape=[
            jax.ShapeDtypeStruct((share, channels), F32),
            jax.ShapeDtypeStruct((share, channels), BF16),
            jax.ShapeDtypeStruct(token.shape, token.dtype),
        ],
        input_output_aliases={1: 2},
        compiler_params=pltpu.CompilerParams(vmem_limit_bytes=VMEM_LIMIT),
        cost_estimate=pl.CostEstimate(
            flops=2 * len(tiles) * rows * width * channels,
            bytes_accessed=2 * len(tiles) * rows * width,
            transcendentals=0,
        ),
        name="section_backward",
    )(*operands)


def sum_fold(near, got, dtype):
    total = near
    for one in got:
        total = total + one.astype(F32)
    return total.astype(dtype)


def grid_of(devices):
    return (4, 2, 2) if devices == 16 else None


def moves(shape):
    zs, ys, cs = shape

    def at(z, y, c):
        return (z * ys + y) * cs + c

    every = [(z, y, c) for z in range(zs) for y in range(ys) for c in range(cs)]
    def pair(bits):
        return [(at(*i), at(i[0] ^ bits, i[1], i[2])) for i in every]

    core = [(at(*i), at(i[0], i[1], i[2] ^ 1)) for i in every]
    row = [(at(*i), at(i[0], i[1] ^ 1, i[2])) for i in every]

    def deep(step):
        return [(at(*i), at((i[0] + step) % zs, i[1], i[2])) for i in every]

    return core, row, deep, pair


def together(*values):
    return lax.optimization_barrier(values)


def send(x, pairs):
    return lax.ppermute(x, "dp", pairs)


def per_device(tiles, conv_weight, tile_slide, slide_owner, labels, attn_v, attn_u, attn_w, class_w):
    tile_count, positions, inputs = tiles.shape
    share, channels = conv_weight.shape
    hidden = attn_v.shape[1]
    classes = class_w.shape[1]
    slides = slide_owner.shape[0]
    devices = lax.axis_size("dp")
    me = lax.axis_index("dp")
    shape = grid_of(devices)
    rows = tile_count * positions
    plain_rows = tiles.reshape(rows, inputs)
    tile_rows = in_hbm(plain_rows)
    lanes = -(-slides // LANES) * LANES
    pad = lanes - slides
    slide = tile_slide[:, None]
    owner = jnp.pad(slide_owner, (0, pad), constant_values=-1)[None, :]
    label = jnp.pad(labels, (0, pad), constant_values=-1)[None, :]
    class_t = class_w.T
    attn_w_row = attn_w[None, :]

    token = jnp.zeros((8, LANES), F32)
    if shape is None:
        where = jnp.zeros((2,), jnp.int32)
        gathered = lax.all_gather(conv_weight, "dp", axis=0, tiled=True)
        mask, pooled, token = forward_chunk(where, token, tile_rows, [gathered], None, True, positions)
    else:
        zs, ys, cs = shape
        core, row, deep, pair = moves(shape)
        z, y, c = me // (ys * cs), me // cs % ys, me % cs
        own_parts, away_parts = [], []

        def block(step, near, pieces):
            spot = (z - step) % zs * ys + (y if near else y ^ 1)
            return spot, pieces

        mine, across, mine_core = conv_weight, send(conv_weight, row), send(conv_weight, core)
        acc, waiting, last = None, [], zs - 1
        for step in range(zs):
            if step < last:
                ahead = send(mine, deep(1))
                extra = []
                if step < 2:
                    extra += split_inputs(c, tile_rows, cs, share, step, 2)
                if step > 0:
                    extra.append(away_parts[step - 1])
                    extra.append(across_core)
                across, ahead, mine_core, token, *extra = together(across, ahead, mine_core, token, *extra)
                if step > 0:
                    landed = extra.pop()
                    if waiting:
                        waiting[-1][1][1] = landed
                    away_parts[step - 1] = in_hbm(extra.pop())
                ahead_across, ahead_core = send(ahead, row), send(ahead, core)
                across_core = send(across, core)
                waiting.append(block(step, True, [mine, mine_core]))
                waiting.append(block(step, False, [across, across_core]))
                if step < 2:
                    own_parts.append(extra[0])
                    if step == 1:
                        across_core, extra[1] = together(across_core, extra[1])
                        waiting[-1] = block(step, False, [across, across_core])
                    away_parts.append(send(extra[1], core))
                if step == last - 1:
                    waiting.append(block(last, True, [ahead, ahead_core]))
                mine, across, mine_core = ahead, ahead_across, ahead_core
            else:
                across, token = together(across, token)
                waiting.append(block(last, False, [across, send(across, core)]))
            if step > 0:
                groups = [spot for spot, _ in waiting]
                order = [i * cs + (c ^ k) for i in range(len(groups)) for k in range(cs)]
                where = jnp.stack([*groups, *order]).astype(jnp.int32)
                pieces = [piece for _, pair in waiting for piece in pair]
                *out, token = forward_chunk(
                    where, token, tile_rows, pieces, acc, step == last, positions, len(groups)
                )
                acc, waiting = out[0], []
        mask, pooled = out

    narrow, wide, packet = score(pooled, slide, attn_v, attn_u, attn_w_row, class_t, lanes)
    narrows, wides, masks = [narrow], [wide], [mask]
    if shape is None:
        boxes = lax.all_gather(packet, "dp", axis=0)
        boxes = [boxes[i] for i in range(devices)]
        where = jnp.stack([me, me, me]).astype(jnp.int32)
    else:
        packet = merge(packet, send(packet, core))
        packet = merge(packet, send(packet, row))
        packet, *ours = together(packet, narrow, wide, mask)
        for group, one in zip((narrows, wides, masks), ours):
            group[0] = one
            group.append(send(one, core))
        boxes = [packet] + [send(packet, deep(i)) for i in (2, 1, 3)]
        where = jnp.stack([me, y, c]).astype(jnp.int32)
    d_pre, term_keep, term_send, logit_rows, loss_rows = grads(
        where, masks, boxes, narrows, wides, owner, label, class_t, slides, shape or (1, 1, 1), positions
    )
    slides_here = slides // devices
    logits = logit_rows[:slides_here, :classes]
    loss = loss_rows[0, :1]

    if shape is None:
        contract = (((0,), (0,)), ((), ()))
        term = lax.dot_general(plain_rows, d_pre, contract, preferred_element_type=F32)
        conv_grad = lax.psum_scatter(term, "dp", scatter_dimension=0, tiled=True)
        pair = lax.psum_scatter(term_keep[:channels], "dp", scatter_dimension=0, tiled=True)
        small = jnp.sum(lax.all_gather(term_keep[channels:], "dp", axis=0), axis=0)
        return (conv_grad, pair[:, :hidden], pair[:, hidden:], small[classes, :hidden], small[:classes].T, logits, loss)

    extra = classes + 1
    steps = (2, 1, 3)
    term_send, token = together(term_send, token)
    attn_got = send(term_send, row)

    where = [jnp.stack([z ^ bits, y, c]).astype(jnp.int32) for bits in range(zs)]

    parts = own_parts + away_parts

    def chunk(bits, d_pre, token):
        near, over, token = backward_chunk(where[bits], token, parts, d_pre, ys, share)
        return near, over, d_pre, token

    near_both, over_both, d_pre, token = chunk(3, d_pre, token)
    over_both, attn_got, token = together(over_both, attn_got, token)
    y_both = send(over_both, row)
    near_far, over_far, d_pre, token = chunk(2, d_pre, token)
    over_far, attn_got, token = together(over_far, attn_got, token)
    y_far = send(over_far, row)
    own, *away = deep_fold(z[None], term_keep, attn_got, steps, extra)
    attn = [send(block, deep(i)) for i, block in zip(steps, away)]
    out_both, token, *_ = together(sum_fold(near_both, [y_both], BF16), token)
    z_both = send(out_both, pair(1))
    near_next, over_next, d_pre, token = chunk(1, d_pre, token)
    over_next, y_far, token, *attn = together(over_next, y_far, token, *attn)
    y_next = send(over_next, row)
    half = share // 48 * 16
    outs = [sum_fold(near_far[at], [y_far[at], z_both[at]], BF16) for at in (slice(half), slice(half, None))]
    *outs, token = together(*outs, token)
    z_far = [send(out, pair(2)) for out in outs]
    near_own, over_own, d_pre, token = chunk(0, d_pre, token)
    over_own, y_next, z_far[0], token = together(over_own, y_next, z_far[0], token)
    y_own = send(over_own, row)
    z_next = send(sum_fold(near_next, [y_next], BF16), pair(1))
    own, z_far[1] = together(own, z_far[1])
    v_grad, u_grad, small = last_fold(own, attn, extra)
    conv_grad = sum_fold(near_own, [y_own, z_next, jnp.concatenate(z_far, axis=0)], F32)
    return (conv_grad, v_grad, u_grad, small[classes, :hidden], small[:classes].T, logits, loss)


def solution(mesh):
    in_specs = (
        P(("groups", "dp"), None, None),
        P("dp", None),
        P(("groups", "dp")),
        P("groups"),
        P("groups"),
        P(),
        P(),
        P(),
        P(),
    )
    out_specs = (
        P(("groups", "dp"), None),
        P(("groups", "dp"), None),
        P(("groups", "dp"), None),
        P("groups"),
        P("groups", None),
        P(("groups", "dp"), None),
        P("groups"),
    )
    return jax.shard_map(per_device, mesh=mesh, in_specs=in_specs, out_specs=out_specs, check_vma=False)
```
